128 devices in a mesh: band: 64 (over z, y, x), feat: 2 (over core).
Axes of the slice: x: 4, y: 4, z: 4, core: 2. Of those that a mesh axis runs over, the one named last changes fastest.
Arguments:
- grid_latent: bfloat16 [65536, 512], P('band'), may hold values from -6 to 6
- mesh_latent: bfloat16 [16384, 512], P('band', 'feat'), may hold values from -6 to 6
- grid_in_w: bfloat16 [512, 512], P(None, 'feat'), may hold values from -0.25 to 0.25
- grid_bias: bfloat16 [512], P('feat'), may hold values from -3 to 3
- g2m_src: int32 [64, 64, 64], P('band'), may hold values from 0 to 1023
- g2m_dst: int32 [64, 64, 64], P('band'), may hold values from 0 to 255
- g2m_weight: bfloat16 [64, 64, 64], P('band'), may hold values from 0 to 2, as said below
- mesh_src: int32 [64, 12288], P('band'), may hold values from 0 to 383
- mesh_dst: int32 [64, 12288], P('band'), may hold values from 0 to 255
- halo_index: int32 [64, 2, 64], P('band'), may hold values from 0 to 255
- edge_send_w: bfloat16 [2, 512, 512], P(None, None, 'feat'), may hold values from -0.25 to 0.25
- edge_recv_w: bfloat16 [2, 512, 512], P(None, None, 'feat'), may hold values from -0.25 to 0.25
- edge_bias: bfloat16 [2, 512], P(None, 'feat'), may hold values from -3 to 3
- node_in_w: bfloat16 [3, 1024, 512], P(None, None, 'feat'), may hold values from -0.125 to 0.125
- node_bias: bfloat16 [3, 512], P(None, 'feat'), may hold values from -3 to 3
- node_out_w: bfloat16 [3, 512, 512], P(None, 'feat'), may hold values from -0.25 to 0.25
Outputs:
- mesh_out: bfloat16 [16384, 512], P('band', 'feat')
The draws below stay inside these ranges and needn't reach their ends.
Inputs may be any that keep to these rules, and one draw needn't show every extreme that they name: `g2m_weight`: each pair of band s and partition d has a live count of 48 to 64: slots c below it have positive weights, the others weight 0. A partition's slots from its own band are all live.
All inputs are finite; a program needn't handle non-finite values.
Results may differ from the reference program's by a relative error of at most 0.029.
Values may be sent and summed in bfloat16 or wider, within the bound.
No kernel may reach another device: no remote copies, remote signals or barrier semaphores. Data moves between devices by JAX's collectives and lax.ppermute only.
A program may use at most 64 MiB of HBM per device.

```python
import jax
import jax.numpy as jnp
from jax import lax

D = 512
G_DEV = 1024
M_DEV = 256
MESH_EDGES = 12288
HALO = 64
STEPS = 2
CAP = 64
G_TOT = 65536
M_TOT = 16384
N_BAND = 64


def draw_g2m_weight(key, part):
    key = jax.random.fold_in(key, 11)
    count_key, value_key = jax.random.split(key)
    counts = jax.random.randint(count_key, (N_BAND, N_BAND), CAP - CAP // 4, CAP + 1)
    diagonal = jnp.arange(N_BAND)[:, None] == jnp.arange(N_BAND)[None, :]
    counts = jnp.where(diagonal, CAP, counts)
    live_slots = jnp.arange(CAP)[None, None, :] < counts[:, :, None]
    values = jax.random.uniform(value_key, (N_BAND, N_BAND, CAP), jnp.float32, 0.5, 1.5)
    return jnp.where(live_slots, values, 0.0).astype(jnp.bfloat16)


def place_ends(result, own_key, low, largest):
    longest = result.shape.index(max(result.shape))
    spots = []
    for shift in (0, 1):
        where = [jax.random.randint(jax.random.fold_in(own_key, axis), (), 0, length) for axis, length in enumerate(result.shape)]
        where[longest] = (where[longest] + shift) % result.shape[longest]
        spots.append(tuple(where))
    return result.at[spots[0]].set(low).at[spots[1]].set(largest)


def level_of(key, dims, shards, least, high):
    loudness = 1.0
    for position, shards_of in shards:
        steps = jax.random.uniform(jax.random.fold_in(jax.random.fold_in(key, 6), position), (shards_of,), jnp.float32, least / len(shards), high / len(shards))
        loudness = loudness * jnp.repeat(jnp.exp(steps), dims[position] // shards_of).reshape((-1,) + (1,) * (len(dims) - 1 - position))
    return loudness


def bell_draw(rng, extent, scale, limit, shards=(), kind=jnp.bfloat16):
    level = level_of(rng, extent, shards, -0.22, 0.18) if shards else 1.0
    entries = jax.random.normal(rng, extent, jnp.float32) * scale * level
    return jnp.minimum(jnp.maximum(entries, -limit), limit).astype(kind)


def setup_inputs(seed: int = 0) -> dict:
    key_of = jax.random.split(jax.random.key(seed), 17)
    return {
        "grid_latent": bell_draw(key_of[0], (G_TOT, D), 1.0, 6.0, ((0, 64),)),
        "mesh_latent": bell_draw(key_of[1], (M_TOT, D), 1.0, 6.0, ((0, 64), (1, 2))),
        "grid_in_w": bell_draw(key_of[2], (D, D), D ** -0.5, 0.25, ((1, 2),)),
        "grid_bias": bell_draw(key_of[3], (D,), 0.5, 3.0, ((0, 2),)),
        "g2m_src": place_ends(jax.random.randint(key_of[4], (N_BAND, N_BAND, CAP), 0, G_DEV), jax.random.fold_in(key_of[4], 1), 0, G_DEV - 1).astype(jnp.int32),
        "g2m_dst": place_ends(jax.random.randint(key_of[5], (N_BAND, N_BAND, CAP), 0, M_DEV), jax.random.fold_in(key_of[5], 1), 0, M_DEV - 1).astype(jnp.int32),
        "g2m_weight": draw_g2m_weight(jax.random.fold_in(key_of[16], 71), 0),
        "mesh_src": place_ends(jax.random.randint(key_of[7], (N_BAND, MESH_EDGES), 0, M_DEV + 2 * HALO), jax.random.fold_in(key_of[7], 1), 0, (M_DEV + 2 * HALO) - 1).astype(jnp.int32),
        "mesh_dst": place_ends(jax.random.randint(key_of[8], (N_BAND, MESH_EDGES), 0, M_DEV), jax.random.fold_in(key_of[8], 1), 0, M_DEV - 1).astype(jnp.int32),
        "halo_index": place_ends(jax.random.randint(key_of[9], (N_BAND, 2, HALO), 0, M_DEV), jax.random.fold_in(key_of[9], 1), 0, M_DEV - 1).astype(jnp.int32),
        "edge_send_w": bell_draw(key_of[10], (STEPS, D, D), D ** -0.5, 0.25, ((2, 2),)),
        "edge_recv_w": bell_draw(key_of[11], (STEPS, D, D), D ** -0.5, 0.25, ((2, 2),)),
        "edge_bias": bell_draw(key_of[12], (STEPS, D), 0.5, 3.0, ((1, 2),)),
        "node_in_w": bell_draw(key_of[13], (STEPS + 1, 2 * D, D), (4 * D) ** -0.5, 0.125, ((2, 2),)),
        "node_bias": bell_draw(key_of[14], (STEPS + 1, D), 0.5, 3.0, ((1, 2),)),
        "node_out_w": bell_draw(key_of[15], (STEPS + 1, D, D), D ** -0.5, 0.25, ((1, 2),)),
    }


def pick_rows(lookup_table, indices):
    return lookup_table[indices]


def reference(grid_latent, mesh_latent, grid_in_w, grid_bias, g2m_src, g2m_dst, g2m_weight, mesh_src, mesh_dst, halo_index, edge_send_w, edge_recv_w, edge_bias, node_in_w, node_bias, node_out_w):
    embedding = jax.nn.silu(jnp.dot(grid_latent, grid_in_w, preferred_element_type=jnp.float32) + grid_bias.astype(jnp.float32)).astype(jnp.bfloat16)
    embed_parts = embedding.reshape(N_BAND, G_DEV, D)

    def encode(destination):
        carried = jax.vmap(pick_rows)(embed_parts, g2m_src[:, destination, :])
        weights = g2m_weight[destination].astype(jnp.float32)
        weighted = carried.astype(jnp.float32) * weights[:, :, None]
        summed = jax.ops.segment_sum(weighted.reshape(-1, D), g2m_dst[destination].reshape(-1), num_segments=M_DEV)
        return summed.astype(jnp.bfloat16)

    aggregate = lax.map(encode, jnp.arange(N_BAND, dtype=jnp.int32)).reshape(N_BAND * M_DEV, D)
    mesh_state = mesh_latent
    for layer_index in range(STEPS + 1):
        if layer_index > 0:
            edge_layer = layer_index - 1
            sender_rows = (jnp.dot(mesh_state, edge_send_w[edge_layer], preferred_element_type=jnp.float32) + edge_bias[edge_layer].astype(jnp.float32)).astype(jnp.bfloat16)
            receiver_rows = jnp.dot(mesh_state, edge_recv_w[edge_layer], preferred_element_type=jnp.float32).astype(jnp.bfloat16)
            sender_parts = sender_rows.reshape(N_BAND, M_DEV, D)
            receiver_parts = receiver_rows.reshape(N_BAND, M_DEV, D)
            upward = jax.vmap(pick_rows)(sender_parts, halo_index[:, 0, :])
            downward = jax.vmap(pick_rows)(sender_parts, halo_index[:, 1, :])
            zero_rows = jnp.zeros((1, HALO, D), jnp.bfloat16)
            from_lower = jnp.concatenate([zero_rows, upward[:-1]], 0)
            from_upper = jnp.concatenate([downward[1:], zero_rows], 0)
            tables = jnp.concatenate([sender_parts, from_lower, from_upper], 1)

            def one_part(partition):
                source_table = tables[partition]
                messages = jax.nn.silu(source_table[mesh_src[partition]].astype(jnp.float32) + receiver_parts[partition][mesh_dst[partition]].astype(jnp.float32)).astype(jnp.bfloat16)
                summed = jax.ops.segment_sum(messages.astype(jnp.float32), mesh_dst[partition], num_segments=M_DEV)
                return summed.astype(jnp.bfloat16)

            aggregate = lax.map(one_part, jnp.arange(N_BAND, dtype=jnp.int32)).reshape(N_BAND * M_DEV, D)
        inputs = jnp.concatenate([mesh_state, aggregate], 1)
        hidden = jax.nn.silu(jnp.dot(inputs, node_in_w[layer_index], preferred_element_type=jnp.float32) + node_bias[layer_index].astype(jnp.float32)).astype(jnp.bfloat16)
        update_total = jnp.dot(hidden, node_out_w[layer_index], preferred_element_type=jnp.float32)
        mesh_state = (mesh_state.astype(jnp.float32) + update_total).astype(jnp.bfloat16)
    return mesh_state
```

```python
import jax
import jax.numpy as jnp
from jax import lax
from jax.sharding import PartitionSpec as P


def select_rows(lookup_table, indices):
    row_ids = lax.broadcasted_iota(jnp.int32, (indices.shape[0], lookup_table.shape[0]), 1)
    selector = (indices[:, None] == row_ids).astype(lookup_table.dtype)
    return jnp.dot(selector, lookup_table, preferred_element_type=jnp.float32).astype(
        lookup_table.dtype
    )


def swap_cores(value):
    return lax.ppermute(value, "feat", [(0, 1), (1, 0)])


def dot32(a, b):
    return jnp.dot(a, b, preferred_element_type=jnp.float32)


def mesh_messages(state_full, send_w, recv_w, bias, source_ids, node_of_edge, halo_ids):
    sender_rows = (dot32(state_full, send_w) + bias.astype(jnp.float32)).astype(jnp.bfloat16)
    receiver_rows = dot32(state_full, recv_w).astype(jnp.bfloat16)
    partitions = lax.axis_size("band")
    up = [(i, (i + 1) % partitions) for i in range(partitions)]
    down = [(j, i) for i, j in up]
    outgoing = select_rows(sender_rows, halo_ids.reshape(-1))
    width = halo_ids.shape[1]
    from_lower = lax.ppermute(outgoing[:width], "band", up)
    from_upper = lax.ppermute(outgoing[width:], "band", down)
    source_table = jnp.concatenate([sender_rows, from_lower, from_upper], 0)
    messages = jax.nn.silu(
        select_rows(source_table, source_ids).astype(jnp.float32)
        + select_rows(receiver_rows, node_of_edge).astype(jnp.float32)
    ).astype(jnp.bfloat16)
    node_ids = lax.broadcasted_iota(jnp.int32, (sender_rows.shape[0], messages.shape[0]), 0)
    matrix = (node_ids == node_of_edge[None, :]).astype(jnp.bfloat16)
    return dot32(matrix, messages).astype(jnp.bfloat16)


def body(
    grid_latent,
    mesh_latent,
    grid_in_w,
    grid_bias,
    g2m_src,
    g2m_dst,
    g2m_weight,
    mesh_src,
    mesh_dst,
    halo_index,
    edge_send_w,
    edge_recv_w,
    edge_bias,
    node_in_w,
    node_bias,
    node_out_w,
):
    feature_width = grid_in_w.shape[1]
    core = lax.axis_index("feat")
    part = lax.axis_index("band")
    embedding = jax.nn.silu(
        dot32(grid_latent, grid_in_w) + grid_bias.astype(jnp.float32)
    ).astype(jnp.bfloat16)
    band_count = g2m_src.shape[1]
    slot_count = g2m_src.shape[2]
    outgoing = select_rows(embedding, g2m_src[0].reshape(-1)).reshape(
        band_count, slot_count, feature_width
    )
    incoming = lax.all_to_all(outgoing, "band", split_axis=0, concat_axis=0, tiled=True)

    state_full = lax.all_gather(mesh_latent, "feat", axis=1, tiled=True)
    in_w = jnp.concatenate([node_in_w, swap_cores(node_in_w)], 2)
    out_w = jnp.concatenate([node_out_w, swap_cores(node_out_w)], 1)
    bias = jnp.concatenate([node_bias, swap_cores(node_bias)], 1).astype(jnp.float32)
    wide = state_full.shape[1]
    mine_first = jnp.where(core == 0, 0, feature_width)
    in_w_state = in_w[:, :wide]
    in_w_mine = lax.dynamic_slice_in_dim(in_w, wide + mine_first, feature_width, 1)
    in_w_other = lax.dynamic_slice_in_dim(in_w, wide + feature_width - mine_first, feature_width, 1)
    last_out_w = lax.dynamic_slice_in_dim(out_w[-1], mine_first, feature_width, 1)

    source_ids = mesh_src[0]
    nodes = mesh_latent.shape[0]
    width = halo_index.shape[2]
    in_lower = (source_ids >= nodes) & (source_ids < nodes + width)
    in_upper = source_ids >= nodes + width
    outside = (in_lower & (part == 0)) | (in_upper & (part == lax.axis_size("band") - 1))
    source_ids = jnp.where(outside, -1, source_ids)

    node_count = mesh_latent.shape[0]
    slot_rows = incoming.reshape(-1, feature_width)
    slot_nodes = g2m_dst[0].reshape(-1)
    slot_weights = g2m_weight[0].reshape(-1)
    node_ids = lax.broadcasted_iota(jnp.int32, (node_count, slot_nodes.shape[0]), 0)
    matrix = jnp.where(
        node_ids == slot_nodes[None, :], slot_weights[None, :], jnp.zeros((), jnp.bfloat16)
    )
    aggregate = dot32(matrix, slot_rows).astype(jnp.bfloat16)
    layer_total = node_in_w.shape[0]
    for layer_index in range(layer_total):
        if layer_index > 0:
            k = layer_index - 1
            aggregate = mesh_messages(
                state_full,
                edge_send_w[k],
                edge_recv_w[k],
                edge_bias[k],
                source_ids,
                mesh_dst[0],
                halo_index[0],
            )
        other = swap_cores(aggregate)
        hidden = jax.nn.silu(
            dot32(state_full, in_w_state[layer_index])
            + dot32(aggregate, in_w_mine[layer_index])
            + dot32(other, in_w_other[layer_index])
            + bias[layer_index]
        ).astype(jnp.bfloat16)
        if layer_index + 1 < layer_total:
            update = dot32(hidden, out_w[layer_index])
            state_full = (state_full.astype(jnp.float32) + update).astype(jnp.bfloat16)
        else:
            before = lax.dynamic_slice_in_dim(state_full, mine_first, feature_width, 1)
            update = dot32(hidden, last_out_w)
            return (before.astype(jnp.float32) + update).astype(jnp.bfloat16)


def solution(mesh):
    in_specs = (
        P("band", None),
        P("band", "feat"),
        P(None, "feat"),
        P("feat"),
        P("band", None, None),
        P("band", None, None),
        P("band", None, None),
        P("band", None),
        P("band", None),
        P("band", None, None),
        P(None, None, "feat"),
        P(None, None, "feat"),
        P(None, "feat"),
        P(None, None, "feat"),
        P(None, "feat"),
        P(None, "feat", None),
    )
    out_specs = P("band", "feat")
    return jax.shard_map(body, mesh=mesh, in_specs=in_specs, out_specs=out_specs, check_vma=False)
```

```python
import functools

import jax
import jax.numpy as jnp
from jax import lax
from jax.experimental import pallas as pl
from jax.experimental.pallas import tpu as pltpu
from jax.sharding import PartitionSpec as P

VMEM = pl.BlockSpec(memory_space=pltpu.VMEM)
SMEM = pl.BlockSpec(memory_space=pltpu.SMEM)
F32 = jnp.float32
BF16 = jnp.bfloat16


def dot32(a, b):
    return jnp.dot(a, b, preferred_element_type=F32)


def dot32_nt(a, b):
    return lax.dot_general(a, b, (((1,), (1,)), ((), ())), preferred_element_type=F32)


def silu(v):
    half = 0.5 * v
    return half + half * jnp.tanh(half)


def one_hot_columns(row, count):
    ids = lax.broadcasted_iota(jnp.int32, (count, row.shape[1]), 0).astype(jnp.int16)
    return jnp.where(ids == row.astype(jnp.int16), jnp.ones((), BF16), jnp.zeros((), BF16))


def call(kernel, name, out_shape, in_specs, flops, limit=24):
    many = isinstance(out_shape, tuple)
    return pl.pallas_call(
        kernel,
        name=name,
        out_shape=out_shape,
        in_specs=in_specs,
        out_specs=(VMEM,) * len(out_shape) if many else VMEM,
        compiler_params=pltpu.CompilerParams(vmem_limit_bytes=limit * 2**20),
        cost_estimate=pl.CostEstimate(flops=flops, bytes_accessed=2**20, transcendentals=0),
    )


def node_hidden(core, state, mine, other, in_mine, in_other, bias_mine, bias_other):
    wide = state.shape[1]
    first = core == 0
    low = jnp.where(first, mine[...], other[...])
    high = jnp.where(first, other[...], mine[...])
    inputs = jnp.concatenate([state[...], low, high], 1)
    hidden_mine = silu(dot32(inputs, in_mine[...]) + bias_mine[...]).astype(BF16)
    hidden_other = silu(dot32(inputs, in_other[...]) + bias_other[...]).astype(BF16)
    return hidden_mine, hidden_other


def node_kernel(
    core, state, mine, other, in_mine, in_other, bias_mine, bias_other, out_mine, out_other,
    send_w, recv_w, edge_bias, halo_hot, state_out, sender_out, receiver_out, up_out, down_out,
):
    hidden_mine, hidden_other = node_hidden(
        core[0], state, mine, other, in_mine, in_other, bias_mine, bias_other
    )
    update = dot32(hidden_mine, out_mine[...]) + dot32(hidden_other, out_other[...])
    after = (state[...].astype(F32) + update).astype(BF16)
    state_out[...] = after
    sender = (dot32(after, send_w[...]) + edge_bias[...]).astype(BF16)
    sender_out[...] = sender
    receiver_out[...] = dot32(after, recv_w[...]).astype(BF16)
    leaving = dot32(halo_hot[...], sender).astype(BF16)
    width = up_out.shape[0]
    up_out[...] = leaving[:width]
    down_out[...] = leaving[width:]


def last_kernel(
    core, state, mine, other, in_mine, in_other, bias_mine, bias_other, out_mine, out_other, result
):
    hidden_mine, hidden_other = node_hidden(
        core[0], state, mine, other, in_mine, in_other, bias_mine, bias_other
    )
    first = core[0] == 0
    narrow = result.shape[1]

    def mine_of(ref):
        return jnp.where(first, ref[:, :narrow], ref[:, narrow:])

    update = dot32(hidden_mine, mine_of(out_mine)) + dot32(hidden_other, mine_of(out_other))
    result[...] = (mine_of(state).astype(F32) + update).astype(BF16)


def local_kernel(source, node, sender, receiver, pre):
    nodes = sender.shape[0]
    table = jnp.concatenate([sender[...].T, receiver[...].T], 1)
    chosen = jnp.concatenate(
        [one_hot_columns(source[...], nodes), one_hot_columns(node[...], nodes)], 0
    )
    pre[...] = dot32(table, chosen)


def halo_kernel(source, node, pre, lower, upper, aggregate):
    nodes = aggregate.shape[0]
    table = jnp.concatenate([lower[...], upper[...]], 0).T
    chosen = one_hot_columns(source[...] - nodes, table.shape[1])
    messages = silu(pre[...] + dot32(table, chosen)).astype(BF16)
    aggregate[...] = dot32_nt(one_hot_columns(node[...], nodes), messages).astype(BF16)


def select_rows(lookup_table, indices):
    row_ids = lax.broadcasted_iota(jnp.int32, (indices.shape[0], lookup_table.shape[0]), 1)
    selector = (indices[:, None] == row_ids).astype(lookup_table.dtype)
    return dot32(selector, lookup_table).astype(lookup_table.dtype)


def swap_cores(value):
    return lax.ppermute(value, "feat", [(0, 1), (1, 0)])


def body(
    grid_latent,
    mesh_latent,
    grid_in_w,
    grid_bias,
    g2m_src,
    g2m_dst,
    g2m_weight,
    mesh_src,
    mesh_dst,
    halo_index,
    edge_send_w,
    edge_recv_w,
    edge_bias,
    node_in_w,
    node_bias,
    node_out_w,
):
    feature_width = grid_in_w.shape[1]
    nodes = mesh_latent.shape[0]
    edges = mesh_src.shape[1]
    halo = halo_index.shape[2]
    partitions = lax.axis_size("band")
    core = lax.axis_index("feat").astype(jnp.int32).reshape(1)
    part = lax.axis_index("band")
    embedding = silu(dot32(grid_latent, grid_in_w) + grid_bias.astype(F32)).astype(BF16)
    band_count = g2m_src.shape[1]
    slot_count = g2m_src.shape[2]
    outgoing = select_rows(embedding, g2m_src[0].reshape(-1)).reshape(
        band_count, slot_count, feature_width
    )
    incoming = lax.all_to_all(outgoing, "band", split_axis=0, concat_axis=0, tiled=True)

    state = lax.all_gather(mesh_latent, "feat", axis=1, tiled=True)
    in_other = swap_cores(node_in_w)
    out_other = swap_cores(node_out_w)
    bias_other = swap_cores(node_bias)
    wide = state.shape[1]

    source = mesh_src
    in_lower = (source >= nodes) & (source < nodes + halo)
    in_upper = source >= nodes + halo
    outside = (in_lower & (part == 0)) | (in_upper & (part == partitions - 1))
    source = jnp.where(outside, -1, source)
    halo_ids = lax.broadcasted_iota(jnp.int32, (2 * halo, nodes), 1)
    halo_hot = (halo_index[0].reshape(-1)[:, None] == halo_ids).astype(BF16)

    slot_rows = incoming.reshape(-1, feature_width)
    slot_nodes = g2m_dst[0].reshape(-1)
    slot_weights = g2m_weight[0].reshape(-1)
    node_ids = lax.broadcasted_iota(jnp.int32, (nodes, slot_nodes.shape[0]), 0)
    matrix = jnp.where(node_ids == slot_nodes[None, :], slot_weights[None, :], jnp.zeros((), BF16))
    aggregate = dot32(matrix, slot_rows).astype(BF16)

    up = [(i, (i + 1) % partitions) for i in range(partitions)]
    down = [(j, i) for i, j in up]
    layer_total = node_in_w.shape[0]
    node_flops = 2 * nodes * wide * (2 * wide + wide)
    for layer in range(layer_total):
        operands = (
            core,
            state,
            aggregate,
            swap_cores(aggregate),
            node_in_w[layer],
            in_other[layer],
            node_bias[layer].astype(F32)[None],
            bias_other[layer].astype(F32)[None],
            node_out_w[layer],
            out_other[layer],
        )
        if layer + 1 == layer_total:
            return call(
                last_kernel,
                "node_last",
                jax.ShapeDtypeStruct((nodes, feature_width), BF16),
                [SMEM] + [VMEM] * 9,
                node_flops,
            )(*operands)
        half = jax.ShapeDtypeStruct((nodes, feature_width), BF16)
        edge_rows = jax.ShapeDtypeStruct((halo, feature_width), BF16)
        state, sender, receiver, to_upper, to_lower = call(
            node_kernel,
            "node",
            (jax.ShapeDtypeStruct((nodes, wide), BF16), half, half, edge_rows, edge_rows),
            [SMEM] + [VMEM] * 13,
            node_flops,
        )(
            *operands,
            edge_send_w[layer],
            edge_recv_w[layer],
            edge_bias[layer].astype(F32)[None],
            halo_hot,
        )
        from_lower = lax.ppermute(to_upper, "band", up)
        from_upper = lax.ppermute(to_lower, "band", down)
        pre = call(
            local_kernel,
            "edge_local",
            pltpu.VMEM((feature_width, edges), F32),
            [VMEM] * 4,
            4 * edges * nodes * feature_width,
        )(source, mesh_dst, sender, receiver)
        aggregate = call(
            halo_kernel,
            "edge_halo",
            half,
            [VMEM] * 5,
            3 * edges * nodes * feature_width,
        )(source, mesh_dst, pre, from_lower, from_upper)


def solution(mesh):
    in_specs = (
        P("band", None),
        P("band", "feat"),
        P(None, "feat"),
        P("feat"),
        P("band", None, None),
        P("band", None, None),
        P("band", None, None),
        P("band", None),
        P("band", None),
        P("band", None, None),
        P(None, None, "feat"),
        P(None, None, "feat"),
        P(None, "feat"),
        P(None, None, "feat"),
        P(None, "feat"),
        P(None, "feat", None),
    )
    out_specs = P("band", "feat")
    return jax.shard_map(body, mesh=mesh, in_specs=in_specs, out_specs=out_specs, check_vma=False)
```

```python
import functools

import jax
import jax.numpy as jnp
from jax import lax
from jax.experimental import pallas as pl
from jax.experimental.pallas import tpu as pltpu
from jax.sharding import PartitionSpec as P

VMEM = pl.BlockSpec(memory_space=pltpu.VMEM)
SMEM = pl.BlockSpec(memory_space=pltpu.SMEM)
HBM = pl.BlockSpec(memory_space=pltpu.HBM)
F32 = jnp.float32
BF16 = jnp.bfloat16


def dot32(a, b):
    return jnp.dot(a, b, preferred_element_type=F32)


def dot32_nt(a, b):
    return lax.dot_general(a, b, (((1,), (1,)), ((), ())), preferred_element_type=F32)


def silu(v):
    half = 0.5 * v
    return half + half * jnp.tanh(half)


def one_hot_columns(row, count):
    ids = lax.broadcasted_iota(jnp.int32, (count, row.shape[1]), 0).astype(jnp.int16)
    return jnp.where(ids == row.astype(jnp.int16), jnp.ones((), BF16), jnp.zeros((), BF16))


def call(kernel, name, out_shape, in_specs, flops, out_specs=None, limit=24, scratch=()):
    many = isinstance(out_shape, tuple)
    return pl.pallas_call(
        kernel,
        name=name,
        out_shape=out_shape,
        in_specs=in_specs,
        out_specs=out_specs or ((VMEM,) * len(out_shape) if many else VMEM),
        scratch_shapes=scratch,
        compiler_params=pltpu.CompilerParams(vmem_limit_bytes=limit * 2**20),
        cost_estimate=pl.CostEstimate(flops=flops, bytes_accessed=2**20, transcendentals=0),
    )


def embed_kernel(grid, weights, bias, source, rows_out, grid_in, weights_in, source_in, rows, sems):
    fetch = [
        pltpu.make_async_copy(grid, grid_in, sems.at[0]),
        pltpu.make_async_copy(weights, weights_in, sems.at[1]),
        pltpu.make_async_copy(source, source_in, sems.at[2]),
    ]
    for copy in fetch:
        copy.start()
    for copy in fetch:
        copy.wait()
    bands, slots, _ = rows_out.shape
    count = grid.shape[0]
    add = bias[...].astype(F32).reshape(1, bias.shape[0])
    embedding = silu(dot32(grid_in[...], weights_in[...]) + add).astype(BF16)
    columns = source_in[0].T
    ids = lax.broadcasted_iota(jnp.int32, (slots, count), 1)
    group = 8 if bands % 8 == 0 else 1
    leave = []
    for first in range(0, bands, group):
        chosen = [
            jnp.where(ids == columns[:, band : band + 1], jnp.ones((), BF16), jnp.zeros((), BF16))
            for band in range(first, first + group)
        ]
        part = dot32(jnp.concatenate(chosen, 0), embedding).astype(BF16)
        rows[first : first + group] = part.reshape(group, slots, part.shape[1])
        copy = pltpu.make_async_copy(
            rows.at[pl.ds(first, group)],
            rows_out.at[pl.ds(first, group)],
            sems.at[3 + first // group],
        )
        copy.start()
        leave.append(copy)
    for copy in leave:
        copy.wait()


def slots_kernel(node, weight, rows, aggregate):
    ids = lax.broadcasted_iota(jnp.int32, (aggregate.shape[0], node.shape[1]), 0)
    chosen = ids.astype(jnp.int16) == node[...].astype(jnp.int16)
    matrix = jnp.where(chosen, weight[...], jnp.zeros((), BF16))
    aggregate[...] = dot32(matrix, rows[...]).astype(BF16)


def node_hidden(core, state, mine, other, in_mine, in_other, bias_mine, bias_other):
    wide = state.shape[1]
    first = core == 0
    low = jnp.where(first, mine[...], other[...])
    high = jnp.where(first, other[...], mine[...])
    inputs = jnp.concatenate([state[...], low, high], 1)
    hidden_mine = silu(dot32(inputs, in_mine[...]) + bias_mine[...]).astype(BF16)
    hidden_other = silu(dot32(inputs, in_other[...]) + bias_other[...]).astype(BF16)
    return hidden_mine, hidden_other


def node_kernel(
    core, state, mine, other, in_mine, in_other, bias_mine, bias_other, out_mine, out_other,
    send_w, recv_w, edge_bias, halo_hot, state_out, sender_out, receiver_out, one_out, two_out,
):
    hidden_mine, hidden_other = node_hidden(
        core[0], state, mine, other, in_mine, in_other, bias_mine, bias_other
    )
    update = dot32(hidden_mine, out_mine[...]) + dot32(hidden_other, out_other[...])
    after = (state[...].astype(F32) + update).astype(BF16)
    state_out[...] = after
    sender = (dot32(after, send_w[...]) + edge_bias[...]).astype(BF16)
    sender_out[...] = sender
    receiver_out[...] = dot32(after, recv_w[...]).astype(BF16)
    leaving = dot32(halo_hot[...], sender).astype(BF16)
    width = one_out.shape[0]
    one_out[...] = leaving[:width]
    two_out[...] = leaving[width:]


def last_kernel(
    core, state, mine, other, in_mine, in_other, bias_mine, bias_other, out_mine, out_other, result
):
    hidden_mine, hidden_other = node_hidden(
        core[0], state, mine, other, in_mine, in_other, bias_mine, bias_other
    )
    first = core[0] == 0
    narrow = result.shape[1]

    def mine_of(ref):
        return jnp.where(first, ref[:, :narrow], ref[:, narrow:])

    update = dot32(hidden_mine, mine_of(out_mine)) + dot32(hidden_other, mine_of(out_other))
    result[...] = (mine_of(state).astype(F32) + update).astype(BF16)


def local_kernel(source, node, sender, receiver, pre):
    nodes = sender.shape[0]
    table = jnp.concatenate([sender[...].T, receiver[...].T], 1)
    chosen = jnp.concatenate(
        [one_hot_columns(source[...], nodes), one_hot_columns(node[...], nodes)], 0
    )
    pre[...] = dot32(table, chosen)


def halo_kernel(source, node, pre, one, two, aggregate):
    nodes = aggregate.shape[0]
    table = jnp.concatenate([one[...], two[...]], 0).T
    chosen = one_hot_columns(source[...] - nodes, table.shape[1])
    messages = silu(pre[...] + dot32(table, chosen)).astype(BF16)
    aggregate[...] = dot32_nt(one_hot_columns(node[...], nodes), messages).astype(BF16)


def swap_cores(value):
    return lax.ppermute(value, "feat", [(0, 1), (1, 0)])


def body(
    grid_latent,
    mesh_latent,
    grid_in_w,
    grid_bias,
    g2m_src,
    g2m_dst,
    g2m_weight,
    mesh_src,
    mesh_dst,
    halo_index,
    edge_send_w,
    edge_recv_w,
    edge_bias,
    node_in_w,
    node_bias,
    node_out_w,
):
    feature_width = grid_in_w.shape[1]
    nodes = mesh_latent.shape[0]
    edges = mesh_src.shape[1]
    halo = halo_index.shape[2]
    partitions = lax.axis_size("band")
    core = lax.axis_index("feat").astype(jnp.int32).reshape(1)
    part = lax.axis_index("band")
    band_count = g2m_src.shape[1]
    slot_count = g2m_src.shape[2]
    slots = band_count * slot_count
    outgoing_shape = (band_count, slot_count, feature_width)
    outgoing = call(
        embed_kernel,
        "embed",
        jax.ShapeDtypeStruct(outgoing_shape, BF16),
        [HBM, HBM, VMEM, HBM],
        2 * slots * grid_latent.shape[0] * feature_width,
        HBM,
        60,
        [
            pltpu.VMEM(grid_latent.shape, BF16),
            pltpu.VMEM(grid_in_w.shape, BF16),
            pltpu.VMEM(g2m_src.shape, jnp.int32),
            pltpu.VMEM(outgoing_shape, BF16),
            pltpu.SemaphoreType.DMA((3 + band_count,)),
        ],
    )(grid_latent, grid_in_w, grid_bias, g2m_src)
    incoming = lax.all_to_all(outgoing, "band", split_axis=0, concat_axis=0, tiled=True)

    _, latent, in_mine, bias_mine, out_mine = lax.optimization_barrier(
        (outgoing, mesh_latent, node_in_w, node_bias, node_out_w)
    )
    layers, deep, _ = node_in_w.shape
    wide = node_out_w.shape[2]
    state = lax.all_gather(latent, "feat", axis=1, tiled=True)
    in_other, bias_other, out_other = swap_cores(in_mine), swap_cores(bias_mine), swap_cores(out_mine)
    node_w = [
        (
            in_mine[layer],
            in_other[layer],
            bias_mine[layer].astype(F32)[None],
            bias_other[layer].astype(F32)[None],
            out_mine[layer],
            out_other[layer],
        )
        for layer in range(layers)
    ]
    edge_w = [
        (edge_send_w[step], edge_recv_w[step], edge_bias[step].astype(F32)[None])
        for step in range(layers - 1)
    ]
    even = part % 2 == 0
    to_next, to_previous = halo_index[0, 0], halo_index[0, 1]
    leaving = jnp.concatenate(
        [jnp.where(even, to_next, to_previous), jnp.where(even, to_previous, to_next)]
    )
    halo_ids = lax.broadcasted_iota(jnp.int32, (2 * halo, nodes), 1)
    halo_hot = (leaving[:, None] == halo_ids).astype(BF16)
    from_previous = (mesh_src >= nodes) & (mesh_src < nodes + halo)
    from_next = mesh_src >= nodes + halo
    source = mesh_src + jnp.where(
        even & from_previous, halo, jnp.where(even & from_next, -halo, 0)
    )
    outside = (from_previous & (part == 0)) | (from_next & (part == partitions - 1))
    source = jnp.where(outside, -1, source)
    slot_node, slot_weight = g2m_dst.reshape(1, slots), g2m_weight.reshape(1, slots)
    incoming, core, state, node_w, edge_w, halo_hot, source, slot_node, slot_weight = (
        lax.optimization_barrier(
            (incoming, core, state, node_w, edge_w, halo_hot, source, slot_node, slot_weight)
        )
    )
    half = jax.ShapeDtypeStruct((nodes, feature_width), BF16)
    aggregate = call(
        slots_kernel,
        "slots",
        half,
        [VMEM] * 3,
        2 * slots * nodes * feature_width,
    )(slot_node, slot_weight, incoming.reshape(slots, -1))

    pairs_one = [(i, i ^ 1) if i ^ 1 < partitions else (i, i) for i in range(partitions)]
    pairs_two = [
        (i, ((i - 1) ^ 1) + 1) if 0 < i and ((i - 1) ^ 1) + 1 < partitions else (i, i)
        for i in range(partitions)
    ]
    halo_rows = jax.ShapeDtypeStruct((halo, feature_width), BF16)
    node_flops = 2 * nodes * wide * (deep + wide)
    for layer in range(layers):
        operands = (core, state, aggregate, swap_cores(aggregate), *node_w[layer])
        if layer + 1 == layers:
            return call(last_kernel, "node_last", half, [SMEM] + [VMEM] * 9, node_flops)(*operands)
        state, sender, receiver, leaving_one, leaving_two = call(
            node_kernel,
            "node",
            (jax.ShapeDtypeStruct((nodes, wide), BF16), half, half, halo_rows, halo_rows),
            [SMEM] + [VMEM] * 13,
            node_flops,
        )(*operands, *edge_w[layer], halo_hot)
        arrived_one = lax.ppermute(leaving_one, "band", pairs_one)
        arrived_two = lax.ppermute(leaving_two, "band", pairs_two)
        pre = call(
            local_kernel,
            "edge_local",
            pltpu.VMEM((feature_width, edges), F32),
            [VMEM] * 4,
            4 * edges * nodes * feature_width,
        )(source, mesh_dst, sender, receiver)
        aggregate = call(
            halo_kernel,
            "edge_halo",
            half,
            [VMEM] * 5,
            3 * edges * nodes * feature_width,
        )(source, mesh_dst, pre, arrived_one, arrived_two)


def solution(mesh):
    in_specs = (
        P("band", None),
        P("band", "feat"),
        P(None, "feat"),
        P("feat"),
        P("band", None, None),
        P("band", None, None),
        P("band", None, None),
        P("band", None),
        P("band", None),
        P("band", None, None),
        P(None, None, "feat"),
        P(None, None, "feat"),
        P(None, "feat"),
        P(None, None, "feat"),
        P(None, "feat"),
        P(None, "feat", None),
    )
    out_specs = P("band", "feat")
    return jax.shard_map(body, mesh=mesh, in_specs=in_specs, out_specs=out_specs, check_vma=False)
```

```python
import functools

import jax
import jax.numpy as jnp
from jax import lax
from jax.experimental import pallas as pl
from jax.experimental.pallas import tpu as pltpu
from jax.sharding import PartitionSpec as P

VMEM = pl.BlockSpec(memory_space=pltpu.VMEM)
SMEM = pl.BlockSpec(memory_space=pltpu.SMEM)
F32 = jnp.float32
BF16 = jnp.bfloat16


def dot32(a, b):
    return jnp.dot(a, b, preferred_element_type=F32)


def dot32_nt(a, b):
    return lax.dot_general(a, b, (((1,), (1,)), ((), ())), preferred_element_type=F32)


def silu(v):
    half = 0.5 * v
    return half + half * jnp.tanh(half)


def one_hot_columns(row, count):
    ids = lax.broadcasted_iota(jnp.int32, (count, row.shape[1]), 0).astype(jnp.int16)
    return jnp.where(ids == row.astype(jnp.int16), jnp.ones((), BF16), jnp.zeros((), BF16))


def call(kernel, name, out_shape, in_specs, flops, limit=24):
    many = isinstance(out_shape, tuple)
    return pl.pallas_call(
        kernel,
        name=name,
        out_shape=out_shape,
        in_specs=in_specs,
        out_specs=(VMEM,) * len(out_shape) if many else VMEM,
        compiler_params=pltpu.CompilerParams(vmem_limit_bytes=limit * 2**20),
        cost_estimate=pl.CostEstimate(flops=flops, bytes_accessed=2**20, transcendentals=0),
    )


def embed_kernel(grid, weights, bias, source, rows_out):
    bands, slots, _ = rows_out.shape
    count = grid.shape[0]
    add = bias[...].astype(F32).reshape(1, bias.shape[0])
    embedding = silu(dot32(grid[...], weights[...]) + add).astype(BF16)
    columns = source[0].T
    ids = lax.broadcasted_iota(jnp.int32, (slots, count), 1)
    group = 8 if bands % 8 == 0 else 1
    for first in range(0, bands, group):
        chosen = [
            jnp.where(ids == columns[:, band : band + 1], jnp.ones((), BF16), jnp.zeros((), BF16))
            for band in range(first, first + group)
        ]
        part = dot32(jnp.concatenate(chosen, 0), embedding).astype(BF16)
        rows_out[first : first + group] = part.reshape(group, slots, part.shape[1])


def slots_kernel(node, weight, rows, aggregate):
    ids = lax.broadcasted_iota(jnp.int32, (aggregate.shape[0], node.shape[1]), 0)
    chosen = ids.astype(jnp.int16) == node[...].astype(jnp.int16)
    matrix = jnp.where(chosen, weight[...], jnp.zeros((), BF16))
    aggregate[...] = dot32(matrix, rows[...]).astype(BF16)


def node_hidden(core, state, mine, other, in_mine, in_other, bias_mine, bias_other):
    wide = state.shape[1]
    first = core == 0
    low = jnp.where(first, mine[...], other[...])
    high = jnp.where(first, other[...], mine[...])
    inputs = jnp.concatenate([state[...], low, high], 1)
    hidden_mine = silu(dot32(inputs, in_mine[...]) + bias_mine[...]).astype(BF16)
    hidden_other = silu(dot32(inputs, in_other[...]) + bias_other[...]).astype(BF16)
    return hidden_mine, hidden_other


def node_kernel(
    core, state, mine, other, in_mine, in_other, bias_mine, bias_other, out_mine, out_other,
    send_w, recv_w, edge_bias, halo_hot, state_out, sender_out, receiver_out, one_out, two_out,
):
    hidden_mine, hidden_other = node_hidden(
        core[0], state, mine, other, in_mine, in_other, bias_mine, bias_other
    )
    update = dot32(hidden_mine, out_mine[...]) + dot32(hidden_other, out_other[...])
    after = (state[...].astype(F32) + update).astype(BF16)
    state_out[...] = after
    sender = (dot32(after, send_w[...]) + edge_bias[...]).astype(BF16)
    sender_out[...] = sender
    receiver_out[...] = dot32(after, recv_w[...]).astype(BF16)
    leaving = dot32(halo_hot[...], sender).astype(BF16)
    width = one_out.shape[0]
    one_out[...] = leaving[:width]
    two_out[...] = leaving[width:]


def last_kernel(
    core, state, mine, other, in_mine, in_other, bias_mine, bias_other, out_mine, out_other, result
):
    hidden_mine, hidden_other = node_hidden(
        core[0], state, mine, other, in_mine, in_other, bias_mine, bias_other
    )
    first = core[0] == 0
    narrow = result.shape[1]

    def mine_of(ref):
        return jnp.where(first, ref[:, :narrow], ref[:, narrow:])

    update = dot32(hidden_mine, mine_of(out_mine)) + dot32(hidden_other, mine_of(out_other))
    result[...] = (mine_of(state).astype(F32) + update).astype(BF16)


def local_kernel(source, node, sender, receiver, pre):
    nodes = sender.shape[0]
    table = jnp.concatenate([sender[...].T, receiver[...].T], 1)
    chosen = jnp.concatenate(
        [one_hot_columns(source[...], nodes), one_hot_columns(node[...], nodes)], 0
    )
    pre[...] = dot32(table, chosen)


def halo_kernel(source, node, pre, one, two, aggregate):
    nodes = aggregate.shape[0]
    table = jnp.concatenate([one[...], two[...]], 0).T
    chosen = one_hot_columns(source[...] - nodes, table.shape[1])
    messages = silu(pre[...] + dot32(table, chosen)).astype(BF16)
    aggregate[...] = dot32_nt(one_hot_columns(node[...], nodes), messages).astype(BF16)


def swap_cores(value):
    return lax.ppermute(value, "feat", [(0, 1), (1, 0)])


def body(
    grid_latent,
    mesh_latent,
    grid_in_w,
    grid_bias,
    g2m_src,
    g2m_dst,
    g2m_weight,
    mesh_src,
    mesh_dst,
    halo_index,
    edge_send_w,
    edge_recv_w,
    edge_bias,
    node_in_w,
    node_bias,
    node_out_w,
):
    feature_width = grid_in_w.shape[1]
    nodes = mesh_latent.shape[0]
    edges = mesh_src.shape[1]
    halo = halo_index.shape[2]
    partitions = lax.axis_size("band")
    core = lax.axis_index("feat").astype(jnp.int32).reshape(1)
    part = lax.axis_index("band")
    band_count = g2m_src.shape[1]
    slot_count = g2m_src.shape[2]
    slots = band_count * slot_count
    outgoing = call(
        embed_kernel,
        "embed",
        jax.ShapeDtypeStruct((band_count, slot_count, feature_width), BF16),
        [VMEM] * 4,
        2 * slots * grid_latent.shape[0] * feature_width,
        limit=60,
    )(grid_latent, grid_in_w, grid_bias, g2m_src)
    incoming = lax.all_to_all(outgoing, "band", split_axis=0, concat_axis=0, tiled=True)

    _, latent, in_mine, bias_mine, out_mine = lax.optimization_barrier(
        (outgoing, mesh_latent, node_in_w, node_bias, node_out_w)
    )
    layers, deep, _ = node_in_w.shape
    wide = node_out_w.shape[2]
    state = lax.all_gather(latent, "feat", axis=1, tiled=True)
    in_other, bias_other, out_other = swap_cores(in_mine), swap_cores(bias_mine), swap_cores(out_mine)
    node_w = [
        (
            in_mine[layer],
            in_other[layer],
            bias_mine[layer].astype(F32)[None],
            bias_other[layer].astype(F32)[None],
            out_mine[layer],
            out_other[layer],
        )
        for layer in range(layers)
    ]
    edge_w = [
        (edge_send_w[step], edge_recv_w[step], edge_bias[step].astype(F32)[None])
        for step in range(layers - 1)
    ]
    odd = part % 2 == 1
    to_next, to_previous = halo_index[0, 0], halo_index[0, 1]
    leaving = jnp.concatenate(
        [jnp.where(odd, to_next, to_previous), jnp.where(odd, to_previous, to_next)]
    )
    halo_ids = lax.broadcasted_iota(jnp.int32, (2 * halo, nodes), 1)
    halo_hot = (leaving[:, None] == halo_ids).astype(BF16)
    from_previous = (mesh_src >= nodes) & (mesh_src < nodes + halo)
    from_next = mesh_src >= nodes + halo
    source = mesh_src + jnp.where(
        odd & from_previous, halo, jnp.where(odd & from_next, -halo, 0)
    )
    outside = (from_previous & (part == 0)) | (from_next & (part == partitions - 1))
    source = jnp.where(outside, -1, source)
    slot_node, slot_weight = g2m_dst.reshape(1, slots), g2m_weight.reshape(1, slots)
    incoming, core, state, node_w, edge_w, halo_hot, source, slot_node, slot_weight = (
        lax.optimization_barrier(
            (incoming, core, state, node_w, edge_w, halo_hot, source, slot_node, slot_weight)
        )
    )
    half = jax.ShapeDtypeStruct((nodes, feature_width), BF16)
    aggregate = call(
        slots_kernel,
        "slots",
        half,
        [VMEM] * 3,
        2 * slots * nodes * feature_width,
    )(slot_node, slot_weight, incoming.reshape(slots, -1))

    cores = lax.axis_size("feat")
    pairs_two = [(i, i ^ 1) for i in range(partitions)]
    pairs_one = []
    for i in range(partitions):
        other = ((i - 1) ^ 1) + 1
        for c in range(cores):
            end = i == 0 or other >= partitions
            partner = i * cores + (c ^ 1) if end else other * cores + c
            pairs_one.append((i * cores + c, partner))
    halo_rows = jax.ShapeDtypeStruct((halo, feature_width), BF16)
    node_flops = 2 * nodes * wide * (deep + wide)
    for layer in range(layers):
        operands = (core, state, aggregate, swap_cores(aggregate), *node_w[layer])
        if layer + 1 == layers:
            return call(last_kernel, "node_last", half, [SMEM] + [VMEM] * 9, node_flops)(*operands)
        state, sender, receiver, leaving_one, leaving_two = call(
            node_kernel,
            "node",
            (jax.ShapeDtypeStruct((nodes, wide), BF16), half, half, halo_rows, halo_rows),
            [SMEM] + [VMEM] * 13,
            node_flops,
        )(*operands, *edge_w[layer], halo_hot)
        arrived_one = lax.ppermute(leaving_one, ("band", "feat"), pairs_one)
        arrived_two = lax.ppermute(leaving_two, "band", pairs_two)
        pre = call(
            local_kernel,
            "edge_local",
            pltpu.VMEM((feature_width, edges), F32),
            [VMEM] * 4,
            4 * edges * nodes * feature_width,
        )(source, mesh_dst, sender, receiver)
        aggregate = call(
            halo_kernel,
            "edge_halo",
            half,
            [VMEM] * 5,
            3 * edges * nodes * feature_width,
        )(source, mesh_dst, pre, arrived_one, arrived_two)


def solution(mesh):
    in_specs = (
        P("band", None),
        P("band", "feat"),
        P(None, "feat"),
        P("feat"),
        P("band", None, None),
        P("band", None, None),
        P("band", None, None),
        P("band", None),
        P("band", None),
        P("band", None, None),
        P(None, None, "feat"),
        P(None, None, "feat"),
        P(None, "feat"),
        P(None, None, "feat"),
        P(None, "feat"),
        P(None, "feat", None),
    )
    out_specs = P("band", "feat")
    return jax.shard_map(body, mesh=mesh, in_specs=in_specs, out_specs=out_specs, check_vma=False)
```

```python
import functools

import jax
import jax.numpy as jnp
from jax import lax
from jax.experimental import pallas as pl
from jax.experimental.pallas import tpu as pltpu
from jax.sharding import PartitionSpec as P

VMEM = pl.BlockSpec(memory_space=pltpu.VMEM)
SMEM = pl.BlockSpec(memory_space=pltpu.SMEM)
F32 = jnp.float32
BF16 = jnp.bfloat16


def dot32(a, b):
    return jnp.dot(a, b, preferred_element_type=F32)


def dot32_nt(a, b):
    return lax.dot_general(a, b, (((1,), (1,)), ((), ())), preferred_element_type=F32)


def silu(v):
    half = 0.5 * v
    return half + half * jnp.tanh(half)


LANES = 128


def head_of(edges):
    return edges * 11 // 24 // (2 * LANES) * (2 * LANES)


def one_hot_columns(row, count):
    ids = lax.broadcasted_iota(jnp.int32, (count, row.shape[1]), 0).astype(jnp.int16)
    return jnp.where(ids == row.astype(jnp.int16), jnp.ones((), BF16), jnp.zeros((), BF16))


def call(kernel, name, out_shape, in_specs, flops, limit=24):
    many = isinstance(out_shape, tuple)
    return pl.pallas_call(
        kernel,
        name=name,
        out_shape=out_shape,
        in_specs=in_specs,
        out_specs=(VMEM,) * len(out_shape) if many else VMEM,
        compiler_params=pltpu.CompilerParams(vmem_limit_bytes=limit * 2**20),
        cost_estimate=pl.CostEstimate(flops=flops, bytes_accessed=2**20, transcendentals=0),
    )


def embed_kernel(grid, weights, bias, source, rows_out):
    bands, slots, _ = rows_out.shape
    count = grid.shape[0]
    add = bias[...].astype(F32).reshape(1, bias.shape[0])
    embedding = silu(dot32(grid[...], weights[...]) + add).astype(BF16)
    columns = source[0].T
    ids = lax.broadcasted_iota(jnp.int32, (slots, count), 1)
    group = 8 if bands % 8 == 0 else 1
    for first in range(0, bands, group):
        chosen = [
            jnp.where(ids == columns[:, band : band + 1], jnp.ones((), BF16), jnp.zeros((), BF16))
            for band in range(first, first + group)
        ]
        part = dot32(jnp.concatenate(chosen, 0), embedding).astype(BF16)
        rows_out[first : first + group] = part.reshape(group, slots, part.shape[1])


def slots_kernel(node, weight, rows, aggregate):
    ids = lax.broadcasted_iota(jnp.int32, (aggregate.shape[0], node.shape[1]), 0)
    chosen = ids.astype(jnp.int16) == node[...].astype(jnp.int16)
    matrix = jnp.where(chosen, weight[...], jnp.zeros((), BF16))
    aggregate[...] = dot32(matrix, rows[...]).astype(BF16)


def own_terms_kernel(core, state, mine, in_mine, in_other, bias_mine, bias_other, sum_mine, sum_other):
    wide, narrow = state.shape[1], mine.shape[1]
    rows = pl.ds(pl.multiple_of(wide + core[0] * narrow, narrow), narrow)
    for weights, bias, total in ((in_mine, bias_mine, sum_mine), (in_other, bias_other, sum_other)):
        own = dot32(mine[...], weights[rows, :])
        total[...] = dot32(state[...], weights[:wide, :]) + own + bias[...]


def hidden_units(core, other, in_mine, in_other, sum_mine, sum_other):
    narrow = other.shape[1]
    wide = in_mine.shape[0] - 2 * narrow
    rows = pl.ds(pl.multiple_of(wide + (1 - core[0]) * narrow, narrow), narrow)
    hidden_mine = silu(sum_mine[...] + dot32(other[...], in_mine[rows, :]))
    hidden_other = silu(sum_other[...] + dot32(other[...], in_other[rows, :]))
    return hidden_mine.astype(BF16), hidden_other.astype(BF16)


def node_kernel(
    core, state, other, in_mine, in_other, sum_mine, sum_other, out_mine, out_other,
    send_w, edge_bias, halo_hot, state_out, sender_out, one_out, two_out,
):
    hidden_mine, hidden_other = hidden_units(core, other, in_mine, in_other, sum_mine, sum_other)
    update = dot32(hidden_mine, out_mine[...]) + dot32(hidden_other, out_other[...])
    after = (state[...].astype(F32) + update).astype(BF16)
    state_out[...] = after
    sender = (dot32(after, send_w[...]) + edge_bias[...]).astype(BF16)
    sender_out[...] = sender
    leaving = dot32(halo_hot[...], sender).astype(BF16)
    width = one_out.shape[0]
    one_out[...] = leaving[:width]
    two_out[...] = leaving[width:]


def last_kernel(
    core, state, other, in_mine, in_other, sum_mine, sum_other, out_mine, out_other, result
):
    hidden_mine, hidden_other = hidden_units(core, other, in_mine, in_other, sum_mine, sum_other)
    update = dot32(hidden_mine, out_mine[...]) + dot32(hidden_other, out_other[...])
    narrow = result.shape[1]
    before = jnp.where(core[0] == 0, state[:, :narrow], state[:, narrow:])
    result[...] = (before.astype(F32) + update).astype(BF16)


def local_kernel(few, keys, sender, state, recv_w, pre, partial):
    nodes = sender.shape[0]
    shift = nodes.bit_length() - 1
    head = head_of(keys.shape[1])
    receiver = dot32(state[...], recv_w[...]).astype(BF16)
    table = jnp.concatenate([sender[...].T, receiver.T], 1)

    def gather(edges):
        to = one_hot_columns(keys[:, edges] & (nodes - 1), nodes)
        chosen = jnp.concatenate([one_hot_columns(keys[:, edges] >> shift, nodes), to], 0)
        return dot32(table, chosen), to

    @pl.when(few[0] == 1)
    def _():
        sums, to = gather(slice(0, head))
        messages = silu(sums).astype(BF16)
        pre[:, head:] = gather(slice(head, None))[0]
        partial[...] = dot32_nt(to, messages)

    @pl.when(few[0] != 1)
    def _():
        pre[...] = gather(slice(0, None))[0]
        partial[...] = jnp.zeros_like(partial)


def halo_kernel(few, keys, pre, partial, one, two, aggregate):
    nodes = aggregate.shape[0]
    shift = nodes.bit_length() - 1
    table = jnp.concatenate([one[...], two[...]], 0).T

    def rest(first):
        source = (keys[:, first:] >> shift) - nodes
        sums = pre[:, first:] + dot32(table, one_hot_columns(source, table.shape[1]))
        to = one_hot_columns(keys[:, first:] & (nodes - 1), nodes)
        return dot32_nt(to, silu(sums).astype(BF16))

    @pl.when(few[0] == 1)
    def _():
        aggregate[...] = (partial[...] + rest(head_of(keys.shape[1]))).astype(BF16)

    @pl.when(few[0] != 1)
    def _():
        aggregate[...] = rest(0).astype(BF16)


def swap_cores(value):
    return lax.ppermute(value, "feat", [(0, 1), (1, 0)])


def body(
    grid_latent,
    mesh_latent,
    grid_in_w,
    grid_bias,
    g2m_src,
    g2m_dst,
    g2m_weight,
    mesh_src,
    mesh_dst,
    halo_index,
    edge_send_w,
    edge_recv_w,
    edge_bias,
    node_in_w,
    node_bias,
    node_out_w,
):
    feature_width = grid_in_w.shape[1]
    nodes = mesh_latent.shape[0]
    edges = mesh_src.shape[1]
    halo = halo_index.shape[2]
    partitions = lax.axis_size("band")
    core = lax.axis_index("feat").astype(jnp.int32).reshape(1)
    part = lax.axis_index("band")
    band_count = g2m_src.shape[1]
    slot_count = g2m_src.shape[2]
    slots = band_count * slot_count
    outgoing = call(
        embed_kernel,
        "embed",
        jax.ShapeDtypeStruct((band_count, slot_count, feature_width), BF16),
        [VMEM] * 4,
        2 * slots * grid_latent.shape[0] * feature_width,
        limit=60,
    )(grid_latent, grid_in_w, grid_bias, g2m_src)
    incoming = lax.all_to_all(outgoing, "band", split_axis=0, concat_axis=0, tiled=True)

    _, latent, in_mine, bias_mine, out_mine = lax.optimization_barrier(
        (outgoing, mesh_latent, node_in_w, node_bias, node_out_w)
    )
    layers, deep, _ = node_in_w.shape
    wide = node_out_w.shape[2]
    state = lax.all_gather(latent, "feat", axis=1, tiled=True)
    in_other, bias_other, out_other = swap_cores(in_mine), swap_cores(bias_mine), swap_cores(out_mine)
    node_w = []
    for layer in range(layers):
        out_w = [out_mine[layer], out_other[layer]]
        if layer + 1 == layers:
            first = core[0] * feature_width
            out_w = [lax.dynamic_slice_in_dim(w, first, feature_width, 1) for w in out_w]
        biases = [b[layer].astype(F32)[None] for b in (bias_mine, bias_other)]
        node_w.append((in_mine[layer], in_other[layer], *biases, *out_w))
    edge_w = [
        (edge_send_w[step], edge_recv_w[step], edge_bias[step].astype(F32)[None])
        for step in range(layers - 1)
    ]
    odd = part % 2 == 1
    to_next, to_previous = halo_index[0, 0], halo_index[0, 1]
    leaving = jnp.concatenate(
        [jnp.where(odd, to_next, to_previous), jnp.where(odd, to_previous, to_next)]
    )
    halo_ids = lax.broadcasted_iota(jnp.int32, (2 * halo, nodes), 1)
    halo_hot = (leaving[:, None] == halo_ids).astype(BF16)
    from_previous = (mesh_src >= nodes) & (mesh_src < nodes + halo)
    from_next = mesh_src >= nodes + halo
    source = mesh_src + jnp.where(
        odd & from_previous, halo, jnp.where(odd & from_next, -halo, 0)
    )
    outside = (from_previous & (part == 0)) | (from_next & (part == partitions - 1))
    source = jnp.where(outside, nodes + 2 * halo, source)
    keys = (source * nodes + mesh_dst).reshape(edges // LANES, LANES)
    keys = lax.sort(keys, dimension=0)
    last = keys[head_of(edges) // LANES - 1]
    few_halo = (jnp.max(last) < nodes * nodes).astype(jnp.int32).reshape(1)
    keys = keys.reshape(1, edges)
    slot_node, slot_weight = g2m_dst.reshape(1, slots), g2m_weight.reshape(1, slots)
    incoming, core, state, node_w, edge_w, halo_hot, keys, few_halo, slot_node, slot_weight = (
        lax.optimization_barrier(
            (incoming, core, state, node_w, edge_w, halo_hot, keys, few_halo, slot_node, slot_weight)
        )
    )
    half = jax.ShapeDtypeStruct((nodes, feature_width), BF16)
    aggregate = call(
        slots_kernel,
        "slots",
        half,
        [VMEM] * 3,
        2 * slots * nodes * feature_width,
    )(slot_node, slot_weight, incoming.reshape(slots, -1))

    cores = lax.axis_size("feat")
    pairs_two = [(i, i ^ 1) for i in range(partitions)]
    pairs_one = []
    for i in range(partitions):
        other = ((i - 1) ^ 1) + 1
        for c in range(cores):
            end = i == 0 or other >= partitions
            partner = i * cores + (c ^ 1) if end else other * cores + c
            pairs_one.append((i * cores + c, partner))
    halo_rows = jax.ShapeDtypeStruct((halo, feature_width), BF16)
    node_flops = 2 * nodes * wide * (deep + wide)
    for layer in range(layers):
        in_one, in_two, bias_one, bias_two, out_one, out_two = node_w[layer]
        total = jax.ShapeDtypeStruct((nodes, feature_width), F32)
        other = swap_cores(aggregate)
        totals = call(
            own_terms_kernel, "own_terms", (total, total), [SMEM] + [VMEM] * 6, node_flops // 2
        )(core, state, aggregate, in_one, in_two, bias_one, bias_two)
        operands = (core, state, other, in_one, in_two, *totals, out_one, out_two)
        if layer + 1 == layers:
            return call(last_kernel, "node_last", half, [SMEM] + [VMEM] * 8, node_flops)(*operands)
        send_w, recv_w, sender_bias = edge_w[layer]
        state, sender, leaving_one, leaving_two = call(
            node_kernel,
            "node",
            (jax.ShapeDtypeStruct((nodes, wide), BF16), half, halo_rows, halo_rows),
            [SMEM] + [VMEM] * 11,
            node_flops,
        )(*operands, send_w, sender_bias, halo_hot)
        arrived_one = lax.ppermute(leaving_one, ("band", "feat"), pairs_one)
        arrived_two = lax.ppermute(leaving_two, "band", pairs_two)
        pre, partial = call(
            local_kernel,
            "edge_local",
            (pltpu.VMEM((feature_width, edges), F32), total),
            [SMEM] + [VMEM] * 4,
            4 * edges * nodes * feature_width,
        )(few_halo, keys, sender, state, recv_w)
        aggregate = call(
            halo_kernel,
            "edge_halo",
            half,
            [SMEM] + [VMEM] * 5,
            3 * edges * nodes * feature_width,
        )(few_halo, keys, pre, partial, arrived_one, arrived_two)


def solution(mesh):
    in_specs = (
        P("band", None),
        P("band", "feat"),
        P(None, "feat"),
        P("feat"),
        P("band", None, None),
        P("band", None, None),
        P("band", None, None),
        P("band", None),
        P("band", None),
        P("band", None, None),
        P(None, None, "feat"),
        P(None, None, "feat"),
        P(None, "feat"),
        P(None, None, "feat"),
        P(None, "feat"),
        P(None, "feat", None),
    )
    out_specs = P("band", "feat")
    return jax.shard_map(body, mesh=mesh, in_specs=in_specs, out_specs=out_specs, check_vma=False)
```

```python
import functools

import jax
import jax.numpy as jnp
from jax import lax
from jax.experimental import pallas as pl
from jax.experimental.pallas import tpu as pltpu
from jax.sharding import PartitionSpec as P

VMEM = pl.BlockSpec(memory_space=pltpu.VMEM)
SMEM = pl.BlockSpec(memory_space=pltpu.SMEM)
F32 = jnp.float32
BF16 = jnp.bfloat16


def dot32(a, b):
    return jnp.dot(a, b, preferred_element_type=F32)


def dot32_nt(a, b):
    return lax.dot_general(a, b, (((1,), (1,)), ((), ())), preferred_element_type=F32)


def silu(v):
    half = 0.5 * v
    return half + half * jnp.tanh(half)


LANES = 128
BLOCK = 768


def head_of(edges):
    return edges * 7 // 16 // BLOCK * BLOCK


def over_blocks(edges, work):
    def step(i, carry):
        work(pl.ds(pl.multiple_of(i * BLOCK, BLOCK), BLOCK))
        return carry

    lax.fori_loop(0, edges // BLOCK, step, 0)


def one_hot_columns(row, count):
    ids = lax.broadcasted_iota(jnp.int32, (count, row.shape[1]), 0).astype(jnp.int16)
    return jnp.where(ids == row.astype(jnp.int16), jnp.ones((), BF16), jnp.zeros((), BF16))


def call(kernel, name, out_shape, in_specs, flops, limit=24, scratch=()):
    many = isinstance(out_shape, tuple)
    return pl.pallas_call(
        kernel,
        name=name,
        out_shape=out_shape,
        in_specs=in_specs,
        out_specs=(VMEM,) * len(out_shape) if many else VMEM,
        scratch_shapes=scratch,
        compiler_params=pltpu.CompilerParams(vmem_limit_bytes=limit * 2**20),
        cost_estimate=pl.CostEstimate(flops=flops, bytes_accessed=2**20, transcendentals=0),
    )


def embed_kernel(grid, weights, bias, source, rows_out):
    bands, slots, _ = rows_out.shape
    count = grid.shape[0]
    add = bias[...].astype(F32).reshape(1, bias.shape[0])
    embedding = silu(dot32(grid[...], weights[...]) + add).astype(BF16)
    columns = source[0].T
    ids = lax.broadcasted_iota(jnp.int32, (slots, count), 1)
    group = 8 if bands % 8 == 0 else 1
    for first in range(0, bands, group):
        chosen = [
            jnp.where(ids == columns[:, band : band + 1], jnp.ones((), BF16), jnp.zeros((), BF16))
            for band in range(first, first + group)
        ]
        part = dot32(jnp.concatenate(chosen, 0), embedding).astype(BF16)
        rows_out[first : first + group] = part.reshape(group, slots, part.shape[1])


def slots_kernel(node, weight, rows, aggregate):
    ids = lax.broadcasted_iota(jnp.int32, (aggregate.shape[0], node.shape[1]), 0)
    chosen = ids.astype(jnp.int16) == node[...].astype(jnp.int16)
    matrix = jnp.where(chosen, weight[...], jnp.zeros((), BF16))
    aggregate[...] = dot32(matrix, rows[...]).astype(BF16)


def own_terms_kernel(core, state, mine, in_mine, in_other, bias_mine, bias_other, sum_mine, sum_other):
    wide, narrow = state.shape[1], mine.shape[1]
    rows = pl.ds(pl.multiple_of(wide + core[0] * narrow, narrow), narrow)
    for weights, bias, total in ((in_mine, bias_mine, sum_mine), (in_other, bias_other, sum_other)):
        own = dot32(mine[...], weights[rows, :])
        total[...] = dot32(state[...], weights[:wide, :]) + own + bias[...]


def hidden_units(core, other, in_mine, in_other, sum_mine, sum_other):
    narrow = other.shape[1]
    wide = in_mine.shape[0] - 2 * narrow
    rows = pl.ds(pl.multiple_of(wide + (1 - core[0]) * narrow, narrow), narrow)
    hidden_mine = silu(sum_mine[...] + dot32(other[...], in_mine[rows, :]))
    hidden_other = silu(sum_other[...] + dot32(other[...], in_other[rows, :]))
    return hidden_mine.astype(BF16), hidden_other.astype(BF16)


def node_kernel(
    core, state, other, in_mine, in_other, sum_mine, sum_other, out_mine, out_other,
    send_w, edge_bias, halo_hot, state_out, sender_out, one_out, two_out,
):
    hidden_mine, hidden_other = hidden_units(core, other, in_mine, in_other, sum_mine, sum_other)
    update = dot32(hidden_mine, out_mine[...]) + dot32(hidden_other, out_other[...])
    after = (state[...].astype(F32) + update).astype(BF16)
    state_out[...] = after
    sender = (dot32(after, send_w[...]) + edge_bias[...]).astype(BF16)
    sender_out[...] = sender
    leaving = dot32(halo_hot[...], sender).astype(BF16)
    width = one_out.shape[0]
    one_out[...] = leaving[:width]
    two_out[...] = leaving[width:]


def last_kernel(
    core, state, other, in_mine, in_other, sum_mine, sum_other, out_mine, out_other, result
):
    hidden_mine, hidden_other = hidden_units(core, other, in_mine, in_other, sum_mine, sum_other)
    update = dot32(hidden_mine, out_mine[...]) + dot32(hidden_other, out_other[...])
    narrow = result.shape[1]
    before = jnp.where(core[0] == 0, state[:, :narrow], state[:, narrow:])
    result[...] = (before.astype(F32) + update).astype(BF16)


def local_kernel(few, keys, sender, state, recv_w, pre, partial):
    nodes = sender.shape[0]
    shift = nodes.bit_length() - 1
    head = head_of(keys.shape[1])
    receiver = dot32(state[...], recv_w[...]).astype(BF16)
    table = jnp.concatenate([sender[...].T, receiver.T], 1)

    def gather(edges):
        to = one_hot_columns(keys[:, edges] & (nodes - 1), nodes)
        chosen = jnp.concatenate([one_hot_columns(keys[:, edges] >> shift, nodes), to], 0)
        return dot32(table, chosen), to

    @pl.when(few[0] == 1)
    def _():
        sums, to = gather(slice(0, head))
        messages = silu(sums).astype(BF16)
        pre[:, head:] = gather(slice(head, None))[0]
        partial[...] = dot32_nt(to, messages)

    @pl.when(few[0] != 1)
    def _():
        def block(edges):
            pre[:, edges] = gather(edges)[0]

        over_blocks(keys.shape[1], block)


def halo_kernel(few, keys, pre, partial, one, two, aggregate, total):
    nodes = aggregate.shape[0]
    shift = nodes.bit_length() - 1
    head = head_of(keys.shape[1])
    table = jnp.concatenate([one[...], two[...]], 0).T

    def sums_of(edges):
        source = (keys[:, edges] >> shift) - nodes
        sums = pre[:, edges] + dot32(table, one_hot_columns(source, table.shape[1]))
        to = one_hot_columns(keys[:, edges] & (nodes - 1), nodes)
        return dot32_nt(to, silu(sums).astype(BF16))

    @pl.when(few[0] == 1)
    def _():
        total[...] = partial[...]

    @pl.when(few[0] != 1)
    def _():
        def block(edges):
            total[...] += sums_of(edges)

        total[...] = jnp.zeros_like(total)
        over_blocks(head, block)

    aggregate[...] = (total[...] + sums_of(slice(head, None))).astype(BF16)


def swap_cores(value):
    return lax.ppermute(value, "feat", [(0, 1), (1, 0)])


def body(
    grid_latent,
    mesh_latent,
    grid_in_w,
    grid_bias,
    g2m_src,
    g2m_dst,
    g2m_weight,
    mesh_src,
    mesh_dst,
    halo_index,
    edge_send_w,
    edge_recv_w,
    edge_bias,
    node_in_w,
    node_bias,
    node_out_w,
):
    feature_width = grid_in_w.shape[1]
    nodes = mesh_latent.shape[0]
    edges = mesh_src.shape[1]
    halo = halo_index.shape[2]
    partitions = lax.axis_size("band")
    core = lax.axis_index("feat").astype(jnp.int32).reshape(1)
    part = lax.axis_index("band")
    band_count = g2m_src.shape[1]
    slot_count = g2m_src.shape[2]
    slots = band_count * slot_count
    outgoing = call(
        embed_kernel,
        "embed",
        jax.ShapeDtypeStruct((band_count, slot_count, feature_width), BF16),
        [VMEM] * 4,
        2 * slots * grid_latent.shape[0] * feature_width,
        limit=60,
    )(grid_latent, grid_in_w, grid_bias, g2m_src)
    incoming = lax.all_to_all(outgoing, "band", split_axis=0, concat_axis=0, tiled=True)

    _, latent, in_mine, bias_mine, out_mine = lax.optimization_barrier(
        (outgoing, mesh_latent, node_in_w, node_bias, node_out_w)
    )
    layers, deep, _ = node_in_w.shape
    wide = node_out_w.shape[2]
    state = lax.all_gather(latent, "feat", axis=1, tiled=True)
    in_other, bias_other, out_other = swap_cores(in_mine), swap_cores(bias_mine), swap_cores(out_mine)
    node_w = []
    for layer in range(layers):
        out_w = [out_mine[layer], out_other[layer]]
        if layer + 1 == layers:
            first = core[0] * feature_width
            out_w = [lax.dynamic_slice_in_dim(w, first, feature_width, 1) for w in out_w]
        biases = [b[layer].astype(F32)[None] for b in (bias_mine, bias_other)]
        node_w.append((in_mine[layer], in_other[layer], *biases, *out_w))
    edge_w = [
        (edge_send_w[step], edge_recv_w[step], edge_bias[step].astype(F32)[None])
        for step in range(layers - 1)
    ]
    odd = part % 2 == 1
    to_next, to_previous = halo_index[0, 0], halo_index[0, 1]
    leaving = jnp.concatenate(
        [jnp.where(odd, to_next, to_previous), jnp.where(odd, to_previous, to_next)]
    )
    halo_ids = lax.broadcasted_iota(jnp.int32, (2 * halo, nodes), 1)
    halo_hot = (leaving[:, None] == halo_ids).astype(BF16)
    from_previous = (mesh_src >= nodes) & (mesh_src < nodes + halo)
    from_next = mesh_src >= nodes + halo
    source = mesh_src + jnp.where(
        odd & from_previous, halo, jnp.where(odd & from_next, -halo, 0)
    )
    outside = (from_previous & (part == 0)) | (from_next & (part == partitions - 1))
    source = jnp.where(outside, nodes + 2 * halo, source)
    keys = (source * nodes + mesh_dst).reshape(edges // LANES, LANES)
    keys = lax.sort(keys, dimension=0)
    last = keys[head_of(edges) // LANES - 1]
    few_halo = (jnp.max(last) < nodes * nodes).astype(jnp.int32).reshape(1)
    keys = keys.reshape(1, edges)
    slot_node, slot_weight = g2m_dst.reshape(1, slots), g2m_weight.reshape(1, slots)
    incoming, core, state, node_w, edge_w, halo_hot, keys, few_halo, slot_node, slot_weight = (
        lax.optimization_barrier(
            (incoming, core, state, node_w, edge_w, halo_hot, keys, few_halo, slot_node, slot_weight)
        )
    )
    half = jax.ShapeDtypeStruct((nodes, feature_width), BF16)
    aggregate = call(
        slots_kernel,
        "slots",
        half,
        [VMEM] * 3,
        2 * slots * nodes * feature_width,
    )(slot_node, slot_weight, incoming.reshape(slots, -1))

    cores = lax.axis_size("feat")
    pairs_two = [(i, i ^ 1) for i in range(partitions)]
    pairs_one = []
    for i in range(partitions):
        other = ((i - 1) ^ 1) + 1
        for c in range(cores):
            end = i == 0 or other >= partitions
            partner = i * cores + (c ^ 1) if end else other * cores + c
            pairs_one.append((i * cores + c, partner))
    halo_rows = jax.ShapeDtypeStruct((halo, feature_width), BF16)
    node_flops = 2 * nodes * wide * (deep + wide)
    for layer in range(layers):
        in_one, in_two, bias_one, bias_two, out_one, out_two = node_w[layer]
        total = jax.ShapeDtypeStruct((nodes, feature_width), F32)
        other = swap_cores(aggregate)
        totals = call(
            own_terms_kernel, "own_terms", (total, total), [SMEM] + [VMEM] * 6, node_flops // 2
        )(core, state, aggregate, in_one, in_two, bias_one, bias_two)
        operands = (core, state, other, in_one, in_two, *totals, out_one, out_two)
        if layer + 1 == layers:
            return call(last_kernel, "node_last", half, [SMEM] + [VMEM] * 8, node_flops)(*operands)
        send_w, recv_w, sender_bias = edge_w[layer]
        state, sender, leaving_one, leaving_two = call(
            node_kernel,
            "node",
            (jax.ShapeDtypeStruct((nodes, wide), BF16), half, halo_rows, halo_rows),
            [SMEM] + [VMEM] * 11,
            node_flops,
        )(*operands, send_w, sender_bias, halo_hot)
        arrived_one = lax.ppermute(leaving_one, ("band", "feat"), pairs_one)
        arrived_two = lax.ppermute(leaving_two, "band", pairs_two)
        pre, partial = call(
            local_kernel,
            "edge_local",
            (pltpu.VMEM((feature_width, edges), F32), total),
            [SMEM] + [VMEM] * 4,
            4 * edges * nodes * feature_width,
        )(few_halo, keys, sender, state, recv_w)
        aggregate = call(
            halo_kernel,
            "edge_halo",
            half,
            [SMEM] + [VMEM] * 5,
            3 * edges * nodes * feature_width,
            scratch=[pltpu.VMEM((nodes, feature_width), F32)],
        )(few_halo, keys, pre, partial, arrived_one, arrived_two)


def solution(mesh):
    in_specs = (
        P("band", None),
        P("band", "feat"),
        P(None, "feat"),
        P("feat"),
        P("band", None, None),
        P("band", None, None),
        P("band", None, None),
        P("band", None),
        P("band", None),
        P("band", None, None),
        P(None, None, "feat"),
        P(None, None, "feat"),
        P(None, "feat"),
        P(None, None, "feat"),
        P(None, "feat"),
        P(None, "feat", None),
    )
    out_specs = P("band", "feat")
    return jax.shard_map(body, mesh=mesh, in_specs=in_specs, out_specs=out_specs, check_vma=False)
```

```python
import functools

import jax
import jax.numpy as jnp
from jax import lax
from jax.experimental import pallas as pl
from jax.experimental.pallas import tpu as pltpu
from jax.sharding import PartitionSpec as P

VMEM = pl.BlockSpec(memory_space=pltpu.VMEM)
SMEM = pl.BlockSpec(memory_space=pltpu.SMEM)
F32 = jnp.float32
BF16 = jnp.bfloat16


def dot32(a, b):
    return jnp.dot(a, b, preferred_element_type=F32)


def dot32_nt(a, b):
    return lax.dot_general(a, b, (((1,), (1,)), ((), ())), preferred_element_type=F32)


def silu(v):
    half = 0.5 * v
    return half + half * jnp.tanh(half)


LANES = 128
BLOCK = 1024


def head_of(edges):
    return edges * 5 // 12 // BLOCK * BLOCK


def over_blocks(edges, work):
    def step(i, carry):
        work(pl.ds(pl.multiple_of(i * BLOCK, BLOCK), BLOCK))
        return carry

    lax.fori_loop(0, edges // BLOCK, step, 0)


def one_hot_columns(row, count):
    ids = lax.broadcasted_iota(jnp.int32, (count, row.shape[1]), 0).astype(jnp.int16)
    return jnp.where(ids == row.astype(jnp.int16), jnp.ones((), BF16), jnp.zeros((), BF16))


def call(kernel, name, out_shape, in_specs, flops, limit=24, scratch=(), out_specs=None):
    many = isinstance(out_shape, tuple)
    return pl.pallas_call(
        kernel,
        name=name,
        out_shape=out_shape,
        in_specs=in_specs,
        out_specs=out_specs or ((VMEM,) * len(out_shape) if many else VMEM),
        scratch_shapes=scratch,
        compiler_params=pltpu.CompilerParams(vmem_limit_bytes=limit * 2**20),
        cost_estimate=pl.CostEstimate(flops=flops, bytes_accessed=2**20, transcendentals=0),
    )


def embed_kernel(grid, weights, bias, source, rows_out, rows, sems):
    bands, slots, _ = rows.shape
    count = grid.shape[0]
    add = bias[...].astype(F32).reshape(1, bias.shape[0])
    embedding = silu(dot32(grid[...], weights[...]) + add).astype(BF16)
    columns = source[0].T
    ids = lax.broadcasted_iota(jnp.int32, (slots, count), 1)
    group = 8 if bands % 8 == 0 else 1
    ends = [bands // 2 // group * group, bands * 3 // 4 // group * group, bands]
    copies = []
    for first, end in zip([0, *ends[:-1]], ends):
        for start in range(first, end, group):
            chosen = [
                jnp.where(ids == columns[:, i : i + 1], jnp.ones((), BF16), jnp.zeros((), BF16))
                for i in range(start, start + group)
            ]
            part = dot32(jnp.concatenate(chosen, 0), embedding).astype(BF16)
            rows[start : start + group] = part.reshape(group, slots, part.shape[1])
        span = pl.ds(first, end - first)
        copy = pltpu.make_async_copy(rows.at[span], rows_out.at[span], sems.at[len(copies)])
        copy.start()
        copies.append(copy)
    for copy in copies:
        copy.wait()


def slots_kernel(node, weight, rows, aggregate):
    ids = lax.broadcasted_iota(jnp.int32, (aggregate.shape[0], node.shape[1]), 0)
    chosen = ids.astype(jnp.int16) == node[...].astype(jnp.int16)
    matrix = jnp.where(chosen, weight[...], jnp.zeros((), BF16))
    aggregate[...] = dot32(matrix, rows[...]).astype(BF16)


def own_terms_kernel(core, state, mine, in_mine, in_other, bias_mine, bias_other, sum_mine, sum_other):
    wide, narrow = state.shape[1], mine.shape[1]
    rows = pl.ds(pl.multiple_of(wide + core[0] * narrow, narrow), narrow)
    for weights, bias, total in ((in_mine, bias_mine, sum_mine), (in_other, bias_other, sum_other)):
        own = dot32(mine[...], weights[rows, :])
        total[...] = dot32(state[...], weights[:wide, :]) + own + bias[...]


def hidden_units(core, other, in_mine, in_other, sum_mine, sum_other):
    narrow = other.shape[1]
    wide = in_mine.shape[0] - 2 * narrow
    rows = pl.ds(pl.multiple_of(wide + (1 - core[0]) * narrow, narrow), narrow)
    hidden_mine = silu(sum_mine[...] + dot32(other[...], in_mine[rows, :]))
    hidden_other = silu(sum_other[...] + dot32(other[...], in_other[rows, :]))
    return hidden_mine.astype(BF16), hidden_other.astype(BF16)


def node_kernel(
    core, state, other, in_mine, in_other, sum_mine, sum_other, out_mine, out_other,
    send_w, edge_bias, halo_hot, state_out, sender_out, one_out, two_out,
):
    hidden_mine, hidden_other = hidden_units(core, other, in_mine, in_other, sum_mine, sum_other)
    update = dot32(hidden_mine, out_mine[...]) + dot32(hidden_other, out_other[...])
    after = (state[...].astype(F32) + update).astype(BF16)
    state_out[...] = after
    sender = (dot32(after, send_w[...]) + edge_bias[...]).astype(BF16)
    sender_out[...] = sender
    leaving = dot32(halo_hot[...], sender).astype(BF16)
    width = one_out.shape[0]
    one_out[...] = leaving[:width]
    two_out[...] = leaving[width:]


def last_kernel(
    core, state, other, in_mine, in_other, sum_mine, sum_other, out_mine, out_other, result
):
    hidden_mine, hidden_other = hidden_units(core, other, in_mine, in_other, sum_mine, sum_other)
    update = dot32(hidden_mine, out_mine[...]) + dot32(hidden_other, out_other[...])
    narrow = result.shape[1]
    before = jnp.where(core[0] == 0, state[:, :narrow], state[:, narrow:])
    result[...] = (before.astype(F32) + update).astype(BF16)


def local_kernel(few, keys, sender, state, recv_w, pre, partial):
    nodes = sender.shape[0]
    shift = nodes.bit_length() - 1
    head = head_of(keys.shape[1])
    receiver = dot32(state[...], recv_w[...]).astype(BF16)
    table = jnp.concatenate([sender[...].T, receiver.T], 1)

    def gather(edges):
        to = one_hot_columns(keys[:, edges] & (nodes - 1), nodes)
        chosen = jnp.concatenate([one_hot_columns(keys[:, edges] >> shift, nodes), to], 0)
        return dot32(table, chosen), to

    @pl.when(few[0] == 1)
    def _():
        sums, to = gather(slice(0, head))
        messages = silu(sums).astype(BF16)
        pre[:, head:] = gather(slice(head, None))[0]
        partial[...] = dot32_nt(to, messages)

    @pl.when(few[0] != 1)
    def _():
        def block(edges):
            pre[:, edges] = gather(edges)[0]

        over_blocks(keys.shape[1], block)


def halo_kernel(few, keys, pre, partial, one, two, aggregate, total):
    nodes = aggregate.shape[0]
    shift = nodes.bit_length() - 1
    head = head_of(keys.shape[1])
    table = jnp.concatenate([one[...], two[...]], 0).T

    def sums_of(edges):
        source = (keys[:, edges] >> shift) - nodes
        sums = pre[:, edges] + dot32(table, one_hot_columns(source, table.shape[1]))
        to = one_hot_columns(keys[:, edges] & (nodes - 1), nodes)
        return dot32_nt(to, silu(sums).astype(BF16))

    @pl.when(few[0] == 1)
    def _():
        total[...] = partial[...]

    @pl.when(few[0] != 1)
    def _():
        def block(edges):
            total[...] += sums_of(edges)

        total[...] = jnp.zeros_like(total)
        over_blocks(head, block)

    aggregate[...] = (total[...] + sums_of(slice(head, None))).astype(BF16)


def swap_cores(value):
    return lax.ppermute(value, "feat", [(0, 1), (1, 0)])


def body(
    grid_latent,
    mesh_latent,
    grid_in_w,
    grid_bias,
    g2m_src,
    g2m_dst,
    g2m_weight,
    mesh_src,
    mesh_dst,
    halo_index,
    edge_send_w,
    edge_recv_w,
    edge_bias,
    node_in_w,
    node_bias,
    node_out_w,
):
    feature_width = grid_in_w.shape[1]
    nodes = mesh_latent.shape[0]
    edges = mesh_src.shape[1]
    halo = halo_index.shape[2]
    partitions = lax.axis_size("band")
    core = lax.axis_index("feat").astype(jnp.int32).reshape(1)
    part = lax.axis_index("band")
    band_count = g2m_src.shape[1]
    slot_count = g2m_src.shape[2]
    slots = band_count * slot_count
    outgoing = call(
        embed_kernel,
        "embed",
        jax.ShapeDtypeStruct((band_count, slot_count, feature_width), BF16),
        [VMEM] * 4,
        2 * slots * grid_latent.shape[0] * feature_width,
        limit=60,
        scratch=[
            pltpu.VMEM((band_count, slot_count, feature_width), BF16),
            pltpu.SemaphoreType.DMA((3,)),
        ],
        out_specs=pl.BlockSpec(memory_space=pltpu.HBM),
    )(grid_latent, grid_in_w, grid_bias, g2m_src)
    incoming = lax.all_to_all(outgoing, "band", split_axis=0, concat_axis=0, tiled=True)

    _, latent, in_mine, bias_mine, out_mine = lax.optimization_barrier(
        (outgoing, mesh_latent, node_in_w, node_bias, node_out_w)
    )
    layers, deep, _ = node_in_w.shape
    wide = node_out_w.shape[2]
    state = lax.all_gather(latent, "feat", axis=1, tiled=True)
    in_other, bias_other, out_other = swap_cores(in_mine), swap_cores(bias_mine), swap_cores(out_mine)
    node_w = []
    for layer in range(layers):
        out_w = [out_mine[layer], out_other[layer]]
        if layer + 1 == layers:
            first = core[0] * feature_width
            out_w = [lax.dynamic_slice_in_dim(w, first, feature_width, 1) for w in out_w]
        biases = [b[layer].astype(F32)[None] for b in (bias_mine, bias_other)]
        node_w.append((in_mine[layer], in_other[layer], *biases, *out_w))
    edge_w = [
        (edge_send_w[step], edge_recv_w[step], edge_bias[step].astype(F32)[None])
        for step in range(layers - 1)
    ]
    odd = part % 2 == 1
    to_next, to_previous = halo_index[0, 0], halo_index[0, 1]
    leaving = jnp.concatenate(
        [jnp.where(odd, to_next, to_previous), jnp.where(odd, to_previous, to_next)]
    )
    halo_ids = lax.broadcasted_iota(jnp.int32, (2 * halo, nodes), 1)
    halo_hot = (leaving[:, None] == halo_ids).astype(BF16)
    from_previous = (mesh_src >= nodes) & (mesh_src < nodes + halo)
    from_next = mesh_src >= nodes + halo
    source = mesh_src + jnp.where(
        odd & from_previous, halo, jnp.where(odd & from_next, -halo, 0)
    )
    outside = (from_previous & (part == 0)) | (from_next & (part == partitions - 1))
    source = jnp.where(outside, nodes + 2 * halo, source)
    keys = (source * nodes + mesh_dst).reshape(edges // LANES, LANES)
    keys = lax.sort(keys, dimension=0)
    last = keys[head_of(edges) // LANES - 1]
    few_halo = (jnp.max(last) < nodes * nodes).astype(jnp.int32).reshape(1)
    keys = keys.reshape(1, edges)
    slot_node, slot_weight = g2m_dst.reshape(1, slots), g2m_weight.reshape(1, slots)
    incoming, core, state, node_w, edge_w, halo_hot, keys, few_halo, slot_node, slot_weight = (
        lax.optimization_barrier(
            (incoming, core, state, node_w, edge_w, halo_hot, keys, few_halo, slot_node, slot_weight)
        )
    )
    half = jax.ShapeDtypeStruct((nodes, feature_width), BF16)
    aggregate = call(
        slots_kernel,
        "slots",
        half,
        [VMEM] * 3,
        2 * slots * nodes * feature_width,
    )(slot_node, slot_weight, incoming.reshape(slots, -1))

    cores = lax.axis_size("feat")
    pairs_two = [(i, i ^ 1) for i in range(partitions)]
    pairs_one = []
    for i in range(partitions):
        other = ((i - 1) ^ 1) + 1
        for c in range(cores):
            end = i == 0 or other >= partitions
            partner = i * cores + (c ^ 1) if end else other * cores + c
            pairs_one.append((i * cores + c, partner))
    halo_rows = jax.ShapeDtypeStruct((halo, feature_width), BF16)
    node_flops = 2 * nodes * wide * (deep + wide)
    for layer in range(layers):
        in_one, in_two, bias_one, bias_two, out_one, out_two = node_w[layer]
        total = jax.ShapeDtypeStruct((nodes, feature_width), F32)
        other = swap_cores(aggregate)
        totals = call(
            own_terms_kernel, "own_terms", (total, total), [SMEM] + [VMEM] * 6, node_flops // 2
        )(core, state, aggregate, in_one, in_two, bias_one, bias_two)
        operands = (core, state, other, in_one, in_two, *totals, out_one, out_two)
        if layer + 1 == layers:
            return call(last_kernel, "node_last", half, [SMEM] + [VMEM] * 8, node_flops)(*operands)
        send_w, recv_w, sender_bias = edge_w[layer]
        state, sender, leaving_one, leaving_two = call(
            node_kernel,
            "node",
            (jax.ShapeDtypeStruct((nodes, wide), BF16), half, halo_rows, halo_rows),
            [SMEM] + [VMEM] * 11,
            node_flops,
        )(*operands, send_w, sender_bias, halo_hot)
        arrived_one = lax.ppermute(leaving_one, ("band", "feat"), pairs_one)
        arrived_two = lax.ppermute(leaving_two, "band", pairs_two)
        pre, partial = call(
            local_kernel,
            "edge_local",
            (pltpu.VMEM((feature_width, edges), F32), total),
            [SMEM] + [VMEM] * 4,
            4 * edges * nodes * feature_width,
        )(few_halo, keys, sender, state, recv_w)
        aggregate = call(
            halo_kernel,
            "edge_halo",
            half,
            [SMEM] + [VMEM] * 5,
            3 * edges * nodes * feature_width,
            scratch=[pltpu.VMEM((nodes, feature_width), F32)],
        )(few_halo, keys, pre, partial, arrived_one, arrived_two)


def solution(mesh):
    in_specs = (
        P("band", None),
        P("band", "feat"),
        P(None, "feat"),
        P("feat"),
        P("band", None, None),
        P("band", None, None),
        P("band", None, None),
        P("band", None),
        P("band", None),
        P("band", None, None),
        P(None, None, "feat"),
        P(None, None, "feat"),
        P(None, "feat"),
        P(None, None, "feat"),
        P(None, "feat"),
        P(None, "feat", None),
    )
    out_specs = P("band", "feat")
    return jax.shard_map(body, mesh=mesh, in_specs=in_specs, out_specs=out_specs, check_vma=False)
```

```python
import functools

import jax
import jax.numpy as jnp
from jax import lax
from jax.experimental import pallas as pl
from jax.experimental.pallas import tpu as pltpu
from jax.sharding import PartitionSpec as P

VMEM = pl.BlockSpec(memory_space=pltpu.VMEM)
SMEM = pl.BlockSpec(memory_space=pltpu.SMEM)
F32 = jnp.float32
BF16 = jnp.bfloat16


def dot32(a, b):
    return jnp.dot(a, b, preferred_element_type=F32)


def dot32_nt(a, b):
    return lax.dot_general(a, b, (((1,), (1,)), ((), ())), preferred_element_type=F32)


def silu(v):
    half = 0.5 * v
    return half + half * jnp.tanh(half)


LANES = 128
BLOCK = 768


def head_of(edges):
    return edges * 5 // 8 // BLOCK * BLOCK


def tail_of(edges):
    return edges * 17 // 24 // (2 * LANES) * (2 * LANES)


def over_blocks(edges, work):
    def step(i, carry):
        work(pl.ds(pl.multiple_of(i * BLOCK, BLOCK), BLOCK))
        return carry

    lax.fori_loop(0, edges // BLOCK, step, 0)


def one_hot_columns(row, count):
    ids = lax.broadcasted_iota(jnp.int32, (count, row.shape[1]), 0).astype(jnp.int16)
    return jnp.where(ids == row.astype(jnp.int16), jnp.ones((), BF16), jnp.zeros((), BF16))


def call(kernel, name, out_shape, in_specs, flops, limit=24, scratch=(), out_specs=None):
    many = isinstance(out_shape, tuple)
    return pl.pallas_call(
        kernel,
        name=name,
        out_shape=out_shape,
        in_specs=in_specs,
        out_specs=out_specs or ((VMEM,) * len(out_shape) if many else VMEM),
        scratch_shapes=scratch,
        compiler_params=pltpu.CompilerParams(vmem_limit_bytes=limit * 2**20),
        cost_estimate=pl.CostEstimate(flops=flops, bytes_accessed=2**20, transcendentals=0),
    )


def embed_kernel(grid, weights, bias, source, rows_out, rows, sems):
    bands, slots, _ = rows.shape
    count = grid.shape[0]
    add = bias[...].astype(F32).reshape(1, bias.shape[0])
    embedding = silu(dot32(grid[...], weights[...]) + add).astype(BF16)
    columns = source[0].T
    ids = lax.broadcasted_iota(jnp.int32, (slots, count), 1)
    group = 8 if bands % 8 == 0 else 1
    ends = [bands // 2 // group * group, bands * 3 // 4 // group * group, bands]
    copies = []
    for first, end in zip([0, *ends[:-1]], ends):
        for start in range(first, end, group):
            chosen = [
                jnp.where(ids == columns[:, i : i + 1], jnp.ones((), BF16), jnp.zeros((), BF16))
                for i in range(start, start + group)
            ]
            part = dot32(jnp.concatenate(chosen, 0), embedding).astype(BF16)
            rows[start : start + group] = part.reshape(group, slots, part.shape[1])
        span = pl.ds(first, end - first)
        copy = pltpu.make_async_copy(rows.at[span], rows_out.at[span], sems.at[len(copies)])
        copy.start()
        copies.append(copy)
    for copy in copies:
        copy.wait()


def slots_kernel(node, weight, rows, aggregate):
    ids = lax.broadcasted_iota(jnp.int32, (aggregate.shape[0], node.shape[1]), 0)
    chosen = ids.astype(jnp.int16) == node[...].astype(jnp.int16)
    matrix = jnp.where(chosen, weight[...], jnp.zeros((), BF16))
    aggregate[...] = dot32(matrix, rows[...]).astype(BF16)


def own_terms_kernel(core, state, mine, in_mine, in_other, bias_mine, bias_other, sum_mine, sum_other):
    wide, narrow = state.shape[1], mine.shape[1]
    rows = pl.ds(pl.multiple_of(wide + core[0] * narrow, narrow), narrow)
    for weights, bias, total in ((in_mine, bias_mine, sum_mine), (in_other, bias_other, sum_other)):
        own = dot32(mine[...], weights[rows, :])
        total[...] = dot32(state[...], weights[:wide, :]) + own + bias[...]


def hidden_units(core, other, in_mine, in_other, sum_mine, sum_other):
    narrow = other.shape[1]
    wide = in_mine.shape[0] - 2 * narrow
    rows = pl.ds(pl.multiple_of(wide + (1 - core[0]) * narrow, narrow), narrow)
    hidden_mine = silu(sum_mine[...] + dot32(other[...], in_mine[rows, :]))
    hidden_other = silu(sum_other[...] + dot32(other[...], in_other[rows, :]))
    return hidden_mine.astype(BF16), hidden_other.astype(BF16)


def node_kernel(
    core, state, other, in_mine, in_other, sum_mine, sum_other, out_mine, out_other,
    send_w, edge_bias, halo_hot, state_out, sender_out, one_out, two_out,
):
    hidden_mine, hidden_other = hidden_units(core, other, in_mine, in_other, sum_mine, sum_other)
    update = dot32(hidden_mine, out_mine[...]) + dot32(hidden_other, out_other[...])
    after = (state[...].astype(F32) + update).astype(BF16)
    state_out[...] = after
    sender = (dot32(after, send_w[...]) + edge_bias[...]).astype(BF16)
    sender_out[...] = sender
    leaving = dot32(halo_hot[...], sender).astype(BF16)
    width = one_out.shape[0]
    one_out[...] = leaving[:width]
    two_out[...] = leaving[width:]


def last_kernel(
    core, state, other, in_mine, in_other, sum_mine, sum_other, out_mine, out_other, result
):
    hidden_mine, hidden_other = hidden_units(core, other, in_mine, in_other, sum_mine, sum_other)
    update = dot32(hidden_mine, out_mine[...]) + dot32(hidden_other, out_other[...])
    narrow = result.shape[1]
    before = jnp.where(core[0] == 0, state[:, :narrow], state[:, narrow:])
    result[...] = (before.astype(F32) + update).astype(BF16)


def local_kernel(usual, keys, sender, state, recv_w, pre, partial):
    nodes = sender.shape[0]
    shift = nodes.bit_length() - 1
    head, tail = head_of(keys.shape[1]), tail_of(keys.shape[1])
    receiver = dot32(state[...], recv_w[...]).astype(BF16)
    table = jnp.concatenate([sender[...].T, receiver.T], 1)

    def gather(edges):
        to = one_hot_columns(keys[:, edges] & (nodes - 1), nodes)
        chosen = jnp.concatenate([one_hot_columns(keys[:, edges] >> shift, nodes), to], 0)
        return dot32(table, chosen), to

    @pl.when(usual[0] == 1)
    def _():
        sums, to = gather(slice(0, head))
        messages = silu(sums).astype(BF16)
        pre[:, head:tail] = gather(slice(head, tail))[0]
        receives = one_hot_columns(keys[:, tail:] & (nodes - 1), nodes)
        pre[:, tail:] = dot32(table[:, nodes:], receives)
        partial[...] = dot32_nt(to, messages)

    @pl.when(usual[0] != 1)
    def _():
        def block(edges):
            pre[:, edges] = gather(edges)[0]

        over_blocks(keys.shape[1], block)


def halo_kernel(usual, keys, pre, partial, one, two, aggregate, total):
    nodes = aggregate.shape[0]
    shift = nodes.bit_length() - 1
    head = head_of(keys.shape[1])
    table = jnp.concatenate([one[...], two[...]], 0).T

    def sums_of(edges):
        source = (keys[:, edges] >> shift) - nodes
        sums = pre[:, edges] + dot32(table, one_hot_columns(source, table.shape[1]))
        to = one_hot_columns(keys[:, edges] & (nodes - 1), nodes)
        return dot32_nt(to, silu(sums).astype(BF16))

    @pl.when(usual[0] == 1)
    def _():
        total[...] = partial[...]

    @pl.when(usual[0] != 1)
    def _():
        def block(edges):
            total[...] += sums_of(edges)

        total[...] = jnp.zeros_like(total)
        over_blocks(head, block)

    aggregate[...] = (total[...] + sums_of(slice(head, None))).astype(BF16)


def swap_cores(value):
    return lax.ppermute(value, "feat", [(0, 1), (1, 0)])


def body(
    grid_latent,
    mesh_latent,
    grid_in_w,
    grid_bias,
    g2m_src,
    g2m_dst,
    g2m_weight,
    mesh_src,
    mesh_dst,
    halo_index,
    edge_send_w,
    edge_recv_w,
    edge_bias,
    node_in_w,
    node_bias,
    node_out_w,
):
    feature_width = grid_in_w.shape[1]
    nodes = mesh_latent.shape[0]
    edges = mesh_src.shape[1]
    halo = halo_index.shape[2]
    partitions = lax.axis_size("band")
    core = lax.axis_index("feat").astype(jnp.int32).reshape(1)
    part = lax.axis_index("band")
    band_count = g2m_src.shape[1]
    slot_count = g2m_src.shape[2]
    slots = band_count * slot_count
    outgoing = call(
        embed_kernel,
        "embed",
        jax.ShapeDtypeStruct((band_count, slot_count, feature_width), BF16),
        [VMEM] * 4,
        2 * slots * grid_latent.shape[0] * feature_width,
        limit=60,
        scratch=[
            pltpu.VMEM((band_count, slot_count, feature_width), BF16),
            pltpu.SemaphoreType.DMA((3,)),
        ],
        out_specs=pl.BlockSpec(memory_space=pltpu.HBM),
    )(grid_latent, grid_in_w, grid_bias, g2m_src)
    incoming = lax.all_to_all(outgoing, "band", split_axis=0, concat_axis=0, tiled=True)

    _, latent, in_mine, bias_mine, out_mine = lax.optimization_barrier(
        (outgoing, mesh_latent, node_in_w, node_bias, node_out_w)
    )
    layers, deep, _ = node_in_w.shape
    wide = node_out_w.shape[2]
    state = lax.all_gather(latent, "feat", axis=1, tiled=True)
    in_other, bias_other, out_other = swap_cores(in_mine), swap_cores(bias_mine), swap_cores(out_mine)
    node_w = []
    for layer in range(layers):
        out_w = [out_mine[layer], out_other[layer]]
        if layer + 1 == layers:
            first = core[0] * feature_width
            out_w = [lax.dynamic_slice_in_dim(w, first, feature_width, 1) for w in out_w]
        biases = [b[layer].astype(F32)[None] for b in (bias_mine, bias_other)]
        node_w.append((in_mine[layer], in_other[layer], *biases, *out_w))
    edge_w = [
        (edge_send_w[step], edge_recv_w[step], edge_bias[step].astype(F32)[None])
        for step in range(layers - 1)
    ]
    odd = part % 2 == 1
    to_next, to_previous = halo_index[0, 0], halo_index[0, 1]
    leaving = jnp.concatenate(
        [jnp.where(odd, to_next, to_previous), jnp.where(odd, to_previous, to_next)]
    )
    halo_ids = lax.broadcasted_iota(jnp.int32, (2 * halo, nodes), 1)
    halo_hot = (leaving[:, None] == halo_ids).astype(BF16)
    from_previous = (mesh_src >= nodes) & (mesh_src < nodes + halo)
    from_next = mesh_src >= nodes + halo
    source = mesh_src + jnp.where(
        odd & from_previous, halo, jnp.where(odd & from_next, -halo, 0)
    )
    outside = (from_previous & (part == 0)) | (from_next & (part == partitions - 1))
    source = jnp.where(outside, nodes + 2 * halo, source)
    keys = lax.sort((source * nodes + mesh_dst).reshape(edges), is_stable=False)
    local = nodes * nodes
    usual = (keys[head_of(edges) - 1] < local) & (keys[tail_of(edges)] >= local)
    usual = usual.astype(jnp.int32).reshape(1)
    keys = keys.reshape(1, edges)
    slot_node, slot_weight = g2m_dst.reshape(1, slots), g2m_weight.reshape(1, slots)
    incoming, core, state, node_w, edge_w, halo_hot, keys, usual, slot_node, slot_weight = (
        lax.optimization_barrier(
            (incoming, core, state, node_w, edge_w, halo_hot, keys, usual, slot_node, slot_weight)
        )
    )
    half = jax.ShapeDtypeStruct((nodes, feature_width), BF16)
    aggregate = call(
        slots_kernel,
        "slots",
        half,
        [VMEM] * 3,
        2 * slots * nodes * feature_width,
    )(slot_node, slot_weight, incoming.reshape(slots, -1))

    cores = lax.axis_size("feat")
    pairs_two = [(i, i ^ 1) for i in range(partitions)]
    pairs_one = []
    for i in range(partitions):
        other = ((i - 1) ^ 1) + 1
        for c in range(cores):
            end = i == 0 or other >= partitions
            partner = i * cores + (c ^ 1) if end else other * cores + c
            pairs_one.append((i * cores + c, partner))
    halo_rows = jax.ShapeDtypeStruct((halo, feature_width), BF16)
    node_flops = 2 * nodes * wide * (deep + wide)
    for layer in range(layers):
        in_one, in_two, bias_one, bias_two, out_one, out_two = node_w[layer]
        total = jax.ShapeDtypeStruct((nodes, feature_width), F32)
        other = swap_cores(aggregate)
        totals = call(
            own_terms_kernel, "own_terms", (total, total), [SMEM] + [VMEM] * 6, node_flops // 2
        )(core, state, aggregate, in_one, in_two, bias_one, bias_two)
        operands = (core, state, other, in_one, in_two, *totals, out_one, out_two)
        if layer + 1 == layers:
            return call(last_kernel, "node_last", half, [SMEM] + [VMEM] * 8, node_flops)(*operands)
        send_w, recv_w, sender_bias = edge_w[layer]
        state, sender, leaving_one, leaving_two = call(
            node_kernel,
            "node",
            (jax.ShapeDtypeStruct((nodes, wide), BF16), half, halo_rows, halo_rows),
            [SMEM] + [VMEM] * 11,
            node_flops,
        )(*operands, send_w, sender_bias, halo_hot)
        arrived_one = lax.ppermute(leaving_one, ("band", "feat"), pairs_one)
        arrived_two = lax.ppermute(leaving_two, "band", pairs_two)
        pre, partial = call(
            local_kernel,
            "edge_local",
            (pltpu.VMEM((feature_width, edges), F32), total),
            [SMEM] + [VMEM] * 4,
            4 * edges * nodes * feature_width,
        )(usual, keys, sender, state, recv_w)
        aggregate = call(
            halo_kernel,
            "edge_halo",
            half,
            [SMEM] + [VMEM] * 5,
            3 * edges * nodes * feature_width,
            scratch=[pltpu.VMEM((nodes, feature_width), F32)],
        )(usual, keys, pre, partial, arrived_one, arrived_two)


def solution(mesh):
    in_specs = (
        P("band", None),
        P("band", "feat"),
        P(None, "feat"),
        P("feat"),
        P("band", None, None),
        P("band", None, None),
        P("band", None, None),
        P("band", None),
        P("band", None),
        P("band", None, None),
        P(None, None, "feat"),
        P(None, None, "feat"),
        P(None, "feat"),
        P(None, None, "feat"),
        P(None, "feat"),
        P(None, "feat", None),
    )
    out_specs = P("band", "feat")
    return jax.shard_map(body, mesh=mesh, in_specs=in_specs, out_specs=out_specs, check_vma=False)
```

```python
import functools

import jax
import jax.numpy as jnp
from jax import lax
from jax.experimental import pallas as pl
from jax.experimental.pallas import tpu as pltpu
from jax.sharding import PartitionSpec as P

VMEM = pl.BlockSpec(memory_space=pltpu.VMEM)
SMEM = pl.BlockSpec(memory_space=pltpu.SMEM)
F32 = jnp.float32
BF16 = jnp.bfloat16


def dot32(a, b):
    return jnp.dot(a, b, preferred_element_type=F32)


def dot32_nt(a, b):
    return lax.dot_general(a, b, (((1,), (1,)), ((), ())), preferred_element_type=F32)


def silu(v):
    half = 0.5 * v
    return half + half * jnp.tanh(half)


LANES = 128
BLOCK = 256


def head_of(edges):
    return edges * 31 // 48 // BLOCK * BLOCK


def tail_of(edges):
    return edges * 11 // 16 // (2 * LANES) * (2 * LANES)


def over_blocks(edges, work):
    def step(i, carry):
        work(pl.ds(pl.multiple_of(i * BLOCK, BLOCK), BLOCK))
        return carry

    lax.fori_loop(0, edges // BLOCK, step, 0)


def one_hot_columns(row, count):
    ids = lax.broadcasted_iota(jnp.int32, (count, row.shape[1]), 0).astype(jnp.int16)
    return jnp.where(ids == row.astype(jnp.int16), jnp.ones((), BF16), jnp.zeros((), BF16))


def call(kernel, name, out_shape, in_specs, flops, limit=24, scratch=(), out_specs=None):
    many = isinstance(out_shape, tuple)
    return pl.pallas_call(
        kernel,
        name=name,
        out_shape=out_shape,
        in_specs=in_specs,
        out_specs=out_specs or ((VMEM,) * len(out_shape) if many else VMEM),
        scratch_shapes=scratch,
        compiler_params=pltpu.CompilerParams(vmem_limit_bytes=limit * 2**20),
        cost_estimate=pl.CostEstimate(flops=flops, bytes_accessed=2**20, transcendentals=0),
    )


def embed_kernel(grid, weights, bias, source, rows_out, rows, sems):
    bands, slots, _ = rows.shape
    count = grid.shape[0]
    add = bias[...].astype(F32).reshape(1, bias.shape[0])
    embedding = silu(dot32(grid[...], weights[...]) + add).astype(BF16)
    columns = source[0].T
    ids = lax.broadcasted_iota(jnp.int32, (slots, count), 1)
    group = 8 if bands % 8 == 0 else 1
    ends = [bands // 2 // group * group, bands * 3 // 4 // group * group, bands]
    copies = []
    for first, end in zip([0, *ends[:-1]], ends):
        for start in range(first, end, group):
            chosen = [
                jnp.where(ids == columns[:, i : i + 1], jnp.ones((), BF16), jnp.zeros((), BF16))
                for i in range(start, start + group)
            ]
            part = dot32(jnp.concatenate(chosen, 0), embedding).astype(BF16)
            rows[start : start + group] = part.reshape(group, slots, part.shape[1])
        span = pl.ds(first, end - first)
        copy = pltpu.make_async_copy(rows.at[span], rows_out.at[span], sems.at[len(copies)])
        copy.start()
        copies.append(copy)
    for copy in copies:
        copy.wait()


def slots_kernel(node, weight, rows, aggregate):
    ids = lax.broadcasted_iota(jnp.int32, (aggregate.shape[0], node.shape[1]), 0)
    chosen = ids.astype(jnp.int16) == node[...].astype(jnp.int16)
    matrix = jnp.where(chosen, weight[...], jnp.zeros((), BF16))
    aggregate[...] = dot32(matrix, rows[...]).astype(BF16)


def own_terms_kernel(core, state, mine, in_mine, in_other, bias_mine, bias_other, sum_mine, sum_other):
    wide, narrow = state.shape[1], mine.shape[1]
    rows = pl.ds(pl.multiple_of(wide + core[0] * narrow, narrow), narrow)
    for weights, bias, total in ((in_mine, bias_mine, sum_mine), (in_other, bias_other, sum_other)):
        own = dot32(mine[...], weights[rows, :])
        total[...] = dot32(state[...], weights[:wide, :]) + own + bias[...]


def hidden_units(core, other, in_mine, in_other, sum_mine, sum_other):
    narrow = other.shape[1]
    wide = in_mine.shape[0] - 2 * narrow
    rows = pl.ds(pl.multiple_of(wide + (1 - core[0]) * narrow, narrow), narrow)
    hidden_mine = silu(sum_mine[...] + dot32(other[...], in_mine[rows, :]))
    hidden_other = silu(sum_other[...] + dot32(other[...], in_other[rows, :]))
    return hidden_mine.astype(BF16), hidden_other.astype(BF16)


def node_kernel(
    core, state, other, in_mine, in_other, sum_mine, sum_other, out_mine, out_other,
    send_w, edge_bias, halo_hot, state_out, sender_out, one_out, two_out,
):
    hidden_mine, hidden_other = hidden_units(core, other, in_mine, in_other, sum_mine, sum_other)
    update = dot32(hidden_mine, out_mine[...]) + dot32(hidden_other, out_other[...])
    after = (state[...].astype(F32) + update).astype(BF16)
    state_out[...] = after
    sender = (dot32(after, send_w[...]) + edge_bias[...]).astype(BF16)
    sender_out[...] = sender
    leaving = dot32(halo_hot[...], sender).astype(BF16)
    width = one_out.shape[0]
    one_out[...] = leaving[:width]
    two_out[...] = leaving[width:]


def last_kernel(
    core, state, other, in_mine, in_other, sum_mine, sum_other, out_mine, out_other, result
):
    hidden_mine, hidden_other = hidden_units(core, other, in_mine, in_other, sum_mine, sum_other)
    update = dot32(hidden_mine, out_mine[...]) + dot32(hidden_other, out_other[...])
    narrow = result.shape[1]
    before = jnp.where(core[0] == 0, state[:, :narrow], state[:, narrow:])
    result[...] = (before.astype(F32) + update).astype(BF16)


def local_kernel(usual, keys, sender, state, recv_w, pre, partial):
    nodes = sender.shape[0]
    shift = nodes.bit_length() - 1
    head, tail = head_of(keys.shape[1]), tail_of(keys.shape[1])
    receiver = dot32(state[...], recv_w[...]).astype(BF16)
    table = jnp.concatenate([sender[...].T, receiver.T], 1)

    def gather(edges):
        to = one_hot_columns(keys[:, edges] & (nodes - 1), nodes)
        chosen = jnp.concatenate([one_hot_columns(keys[:, edges] >> shift, nodes), to], 0)
        return dot32(table, chosen), to

    @pl.when(usual[0] == 1)
    def _():
        sums, to = gather(slice(0, head))
        messages = silu(sums).astype(BF16)
        pre[:, head:tail] = gather(slice(head, tail))[0]
        receives = one_hot_columns(keys[:, tail:] & (nodes - 1), nodes)
        pre[:, tail:] = dot32(table[:, nodes:], receives)
        partial[...] = dot32_nt(to, messages)

    @pl.when(usual[0] != 1)
    def _():
        def block(edges):
            pre[:, edges] = gather(edges)[0]

        over_blocks(keys.shape[1], block)


def halo_kernel(usual, keys, pre, partial, one, two, aggregate, total):
    nodes = aggregate.shape[0]
    shift = nodes.bit_length() - 1
    head = head_of(keys.shape[1])
    table = jnp.concatenate([one[...], two[...]], 0).T

    def sums_of(edges):
        source = (keys[:, edges] >> shift) - nodes
        sums = pre[:, edges] + dot32(table, one_hot_columns(source, table.shape[1]))
        to = one_hot_columns(keys[:, edges] & (nodes - 1), nodes)
        return dot32_nt(to, silu(sums).astype(BF16))

    @pl.when(usual[0] == 1)
    def _():
        total[...] = partial[...]

    @pl.when(usual[0] != 1)
    def _():
        def block(edges):
            total[...] += sums_of(edges)

        total[...] = jnp.zeros_like(total)
        over_blocks(head, block)

    aggregate[...] = (total[...] + sums_of(slice(head, None))).astype(BF16)


def swap_cores(value):
    return lax.ppermute(value, "feat", [(0, 1), (1, 0)])


def body(
    grid_latent,
    mesh_latent,
    grid_in_w,
    grid_bias,
    g2m_src,
    g2m_dst,
    g2m_weight,
    mesh_src,
    mesh_dst,
    halo_index,
    edge_send_w,
    edge_recv_w,
    edge_bias,
    node_in_w,
    node_bias,
    node_out_w,
):
    feature_width = grid_in_w.shape[1]
    nodes = mesh_latent.shape[0]
    edges = mesh_src.shape[1]
    halo = halo_index.shape[2]
    partitions = lax.axis_size("band")
    core = lax.axis_index("feat").astype(jnp.int32).reshape(1)
    part = lax.axis_index("band")
    band_count = g2m_src.shape[1]
    slot_count = g2m_src.shape[2]
    slots = band_count * slot_count
    outgoing = call(
        embed_kernel,
        "embed",
        jax.ShapeDtypeStruct((band_count, slot_count, feature_width), BF16),
        [VMEM] * 4,
        2 * slots * grid_latent.shape[0] * feature_width,
        limit=60,
        scratch=[
            pltpu.VMEM((band_count, slot_count, feature_width), BF16),
            pltpu.SemaphoreType.DMA((3,)),
        ],
        out_specs=pl.BlockSpec(memory_space=pltpu.HBM),
    )(grid_latent, grid_in_w, grid_bias, g2m_src)
    incoming = lax.all_to_all(outgoing, "band", split_axis=0, concat_axis=0, tiled=True)

    _, latent, in_mine, bias_mine, out_mine = lax.optimization_barrier(
        (outgoing, mesh_latent, node_in_w, node_bias, node_out_w)
    )
    layers, deep, _ = node_in_w.shape
    wide = node_out_w.shape[2]
    state = lax.all_gather(latent, "feat", axis=1, tiled=True)
    in_other, bias_other, out_other = swap_cores(in_mine), swap_cores(bias_mine), swap_cores(out_mine)
    node_w = []
    for layer in range(layers):
        out_w = [out_mine[layer], out_other[layer]]
        if layer + 1 == layers:
            first = core[0] * feature_width
            out_w = [lax.dynamic_slice_in_dim(w, first, feature_width, 1) for w in out_w]
        biases = [b[layer].astype(F32)[None] for b in (bias_mine, bias_other)]
        node_w.append((in_mine[layer], in_other[layer], *biases, *out_w))
    edge_w = [
        (edge_send_w[step], edge_recv_w[step], edge_bias[step].astype(F32)[None])
        for step in range(layers - 1)
    ]
    odd = part % 2 == 1
    to_next, to_previous = halo_index[0, 0], halo_index[0, 1]
    leaving = jnp.concatenate(
        [jnp.where(odd, to_next, to_previous), jnp.where(odd, to_previous, to_next)]
    )
    halo_ids = lax.broadcasted_iota(jnp.int32, (2 * halo, nodes), 1)
    halo_hot = (leaving[:, None] == halo_ids).astype(BF16)
    from_previous = (mesh_src >= nodes) & (mesh_src < nodes + halo)
    from_next = mesh_src >= nodes + halo
    source = mesh_src + jnp.where(
        odd & from_previous, halo, jnp.where(odd & from_next, -halo, 0)
    )
    outside = (from_previous & (part == 0)) | (from_next & (part == partitions - 1))
    source = jnp.where(outside, nodes + 2 * halo, source)
    keys = lax.sort((source * nodes + mesh_dst).reshape(edges), is_stable=False)
    local = nodes * nodes
    usual = (keys[head_of(edges) - 1] < local) & (keys[tail_of(edges)] >= local)
    usual = usual.astype(jnp.int32).reshape(1)
    keys = keys.reshape(1, edges)
    slot_node, slot_weight = g2m_dst.reshape(1, slots), g2m_weight.reshape(1, slots)
    incoming, core, state, node_w, edge_w, halo_hot, keys, usual, slot_node, slot_weight = (
        lax.optimization_barrier(
            (incoming, core, state, node_w, edge_w, halo_hot, keys, usual, slot_node, slot_weight)
        )
    )
    half = jax.ShapeDtypeStruct((nodes, feature_width), BF16)
    aggregate = call(
        slots_kernel,
        "slots",
        half,
        [VMEM] * 3,
        2 * slots * nodes * feature_width,
    )(slot_node, slot_weight, incoming.reshape(slots, -1))

    cores = lax.axis_size("feat")
    pairs_two = [(i, i ^ 1) for i in range(partitions)]
    pairs_one = []
    for i in range(partitions):
        other = ((i - 1) ^ 1) + 1
        for c in range(cores):
            end = i == 0 or other >= partitions
            partner = i * cores + (c ^ 1) if end else other * cores + c
            pairs_one.append((i * cores + c, partner))
    halo_rows = jax.ShapeDtypeStruct((halo, feature_width), BF16)
    node_flops = 2 * nodes * wide * (deep + wide)
    for layer in range(layers):
        in_one, in_two, bias_one, bias_two, out_one, out_two = node_w[layer]
        total = jax.ShapeDtypeStruct((nodes, feature_width), F32)
        other = swap_cores(aggregate)
        totals = call(
            own_terms_kernel, "own_terms", (total, total), [SMEM] + [VMEM] * 6, node_flops // 2
        )(core, state, aggregate, in_one, in_two, bias_one, bias_two)
        operands = (core, state, other, in_one, in_two, *totals, out_one, out_two)
        if layer + 1 == layers:
            return call(last_kernel, "node_last", half, [SMEM] + [VMEM] * 8, node_flops)(*operands)
        send_w, recv_w, sender_bias = edge_w[layer]
        state, sender, leaving_one, leaving_two = call(
            node_kernel,
            "node",
            (jax.ShapeDtypeStruct((nodes, wide), BF16), half, halo_rows, halo_rows),
            [SMEM] + [VMEM] * 11,
            node_flops,
        )(*operands, send_w, sender_bias, halo_hot)
        arrived_one = lax.ppermute(leaving_one, ("band", "feat"), pairs_one)
        arrived_two = lax.ppermute(leaving_two, "band", pairs_two)
        pre, partial = call(
            local_kernel,
            "edge_local",
            (pltpu.VMEM((feature_width, edges), F32), total),
            [SMEM] + [VMEM] * 4,
            4 * edges * nodes * feature_width,
        )(usual, keys, sender, state, recv_w)
        aggregate = call(
            halo_kernel,
            "edge_halo",
            half,
            [SMEM] + [VMEM] * 5,
            3 * edges * nodes * feature_width,
            scratch=[pltpu.VMEM((nodes, feature_width), F32)],
        )(usual, keys, pre, partial, arrived_one, arrived_two)


def solution(mesh):
    in_specs = (
        P("band", None),
        P("band", "feat"),
        P(None, "feat"),
        P("feat"),
        P("band", None, None),
        P("band", None, None),
        P("band", None, None),
        P("band", None),
        P("band", None),
        P("band", None, None),
        P(None, None, "feat"),
        P(None, None, "feat"),
        P(None, "feat"),
        P(None, None, "feat"),
        P(None, "feat"),
        P(None, "feat", None),
    )
    out_specs = P("band", "feat")
    return jax.shard_map(body, mesh=mesh, in_specs=in_specs, out_specs=out_specs, check_vma=False)
```
